32 devices in a mesh: leaf: 32 (over z, y, x, core).
Axes of the slice: x: 2, y: 2, z: 4, core: 2. Of those that a mesh axis runs over, the one named last changes fastest.
Arguments:
- points: bfloat16 [16, 262144], P(None, 'leaf'), may hold values from -6 to 6
- coords: float32 [3, 262144], P(None, 'leaf'), may hold values from 0 to 1, as said below
- basis: bfloat16 [4096, 2048], P('leaf'), may hold values from -0.75 to 0.75
- far_list: int32 [4096, 16], P('leaf'), may hold values from -1 to 4095, as said below
- far_coupling: bfloat16 [4096, 16, 1024], P('leaf'), may hold values from -0.25 to 0.25
- near_list: int32 [4096, 12], P('leaf'), may hold values from -1 to 4095, as said below
- local_transfer: bfloat16 [8128, 1024], P('leaf'), may hold values from -0.875 to 0.875
- top_transfer: bfloat16 [62, 1024], replicated, may hold values from -0.875 to 0.875
- top_coupling: bfloat16 [60, 2, 1024], replicated, may hold values from -0.75 to 0.75
Outputs:
- product: float32 [16, 262144], P(None, 'leaf')
The draws below stay inside these ranges and needn't reach their ends.
Inputs may be any that keep to these rules, and one draw needn't show every extreme that they name: `far_list`: -1 marks an empty slot; every other entry is a leaf of the leaf's own device or of a device whose index differs from it in exactly one bit (devices hold 128 leaves each, in order). `near_list`: -1 marks an empty slot; slot 0 holds the leaf itself; every other entry is another leaf at most 8 positions away from it in leaf order. `coords`: the points of leaf i lie in cell i of a k-d split of the unit cube that halves x, y, z in turn, by the bits of i from the most significant.
All inputs are finite; a program needn't handle non-finite values.
Results may differ from the reference program's by a relative error of at most 0.0013.
The reference program's roundings to bfloat16 on the way (of `leaf_coeff` and `kernel`) count: a program that leaves them out, or rounds other values in their place, can miss the bound.
Values may be sent and summed in bfloat16 or wider, within the bound.
A program may use at most 128 MiB of HBM per device.

```python
import math
import jax
import jax.numpy as jnp
from jax import lax

R = 16
LEAF = 64
RANK = 32
LEAF_DEV = 128
NF = 16
NN = 12
SPAN = 8
LEAVES = 4096
N = 262144
N_LEAF = 32


def draw_coords(key, part):
    key = jax.random.fold_in(key, 13)
    bit_total = LEAVES.bit_length() - 1
    leaf_ids = jnp.arange(N, dtype=jnp.int32) // LEAF
    cells = [jnp.zeros((N,), jnp.int32) for component in range(3)]
    splits = [0, 0, 0]
    for bit_num in range(bit_total):
        component = bit_num % 3
        bit_value = jnp.bitwise_and(jnp.right_shift(leaf_ids, bit_total - 1 - bit_num), 1)
        cells[component] = cells[component] * 2 + bit_value
        splits[component] += 1
    inside = jax.random.uniform(key, (3, N), jnp.float32, 0.0, 1.0)
    rows = []
    for component in range(3):
        side = 1.0 / float(2 ** splits[component])
        rows.append((cells[component].astype(jnp.float32) + inside[component]) * side)
    return jnp.clip(jnp.stack(rows), 0.0, 1.0).astype(jnp.float32)


def draw_far_list(key, part):
    key = jax.random.fold_in(key, 11)
    key_count, key_opening, key_within = jax.random.split(key, 3)
    device_total = LEAVES // LEAF_DEV
    tree_bits = device_total.bit_length() - 1
    leaf_ids = jnp.arange(LEAVES, dtype=jnp.int32)
    owner = leaf_ids // LEAF_DEV
    filled = jax.random.randint(key_count, (LEAVES, 1), NF // 2, NF + 1)
    opening = jax.random.randint(key_opening, (LEAVES, 1), 0, tree_bits + 1)
    slot_ids = jnp.arange(NF, dtype=jnp.int32)[None, :]
    choose_bit = (opening + slot_ids) % (tree_bits + 1)
    flips = jnp.where(choose_bit < tree_bits, jnp.left_shift(jnp.ones_like(choose_bit), choose_bit), 0)
    partner_device = jnp.bitwise_xor(owner[:, None], flips)
    within = jax.random.randint(key_within, (LEAVES, NF), 0, LEAF_DEV)
    return jnp.where(slot_ids < filled, partner_device * LEAF_DEV + within, -1).astype(jnp.int32)


def draw_near_list(key, part):
    key = jax.random.fold_in(key, 12)
    key_count, key_reach, key_heading = jax.random.split(key, 3)
    leaf_ids = jnp.arange(LEAVES, dtype=jnp.int32)
    filled = jax.random.randint(key_count, (LEAVES, 1), 3, NN + 1)
    reach = jax.random.randint(key_reach, (LEAVES, NN), 1, SPAN + 1)
    heading = jax.random.randint(key_heading, (LEAVES, NN), 0, 2) * 2 - 1
    target = leaf_ids[:, None] + reach * heading
    slot_ids = jnp.arange(NN, dtype=jnp.int32)[None, :]
    target = jnp.where(slot_ids == 1, leaf_ids[:, None] + SPAN, target)
    target = jnp.where(slot_ids == 2, leaf_ids[:, None] - SPAN, target)
    usable = (slot_ids < filled) & (target >= 0) & (target < LEAVES)
    result = jnp.where(usable, target, -1)
    result = jnp.where(slot_ids == 0, leaf_ids[:, None], result)
    return result.astype(jnp.int32)


def level_of(own_key, extent, shards, smallest, largest):
    factor_of = 1.0
    for axis_at, shards_of in shards:
        steps = jax.random.uniform(jax.random.fold_in(jax.random.fold_in(own_key, 6), axis_at), (shards_of,), jnp.float32, smallest / len(shards), largest / len(shards))
        factor_of = factor_of * jnp.repeat(jnp.exp(steps), extent[axis_at] // shards_of).reshape((-1,) + (1,) * (len(extent) - 1 - axis_at))
    return factor_of


def scatter_about(stream_key, dims, deviation, most, shards=(), kind=jnp.bfloat16):
    values = deviation * jax.random.normal(stream_key, dims, jnp.float32)
    if shards:
        values = values * level_of(stream_key, dims, shards, -0.22, 0.18)
    return jnp.clip(values, -most, most).astype(kind)


def setup_inputs(seed: int = 0) -> dict:
    key_list = jax.random.split(jax.random.key(seed), 10)
    points = scatter_about(key_list[0], (R, N), 1.0, 6.0, ((1, 32),))
    coords = draw_coords(jax.random.fold_in(key_list[9], 71), 0)
    basis = scatter_about(key_list[2], (LEAVES, LEAF * RANK), LEAF ** -0.5, 0.75, ((0, 32),))
    far_list = draw_far_list(jax.random.fold_in(key_list[9], 71), 0)
    far_coupling = scatter_about(key_list[4], (LEAVES, NF, RANK * RANK), (RANK * NF) ** -0.5, 0.25, ((0, 32),))
    near_list = draw_near_list(jax.random.fold_in(key_list[9], 71), 0)
    local_transfer = scatter_about(key_list[6], (N_LEAF * (2 * LEAF_DEV - 2), RANK * RANK), (3 * RANK // 2) ** -0.5, 0.875, ((0, 32),))
    top_transfer = scatter_about(key_list[7], (2 * N_LEAF - 2, RANK * RANK), (3 * RANK // 2) ** -0.5, 0.875)
    top_coupling = scatter_about(key_list[8], (2 * N_LEAF - 4, 2, RANK * RANK), (2 * RANK) ** -0.5, 0.75)
    return dict(points=points, coords=coords, basis=basis, far_list=far_list, far_coupling=far_coupling, near_list=near_list, local_transfer=local_transfer, top_transfer=top_transfer, top_coupling=top_coupling)


variance = 1.0
nugget = 0.5
decay_rate = math.sqrt(3.0) / 0.3
highest = lax.Precision.HIGHEST

def matern_block(own_coords, part_coords, own_ids, part_ids, present):
    width = own_coords.shape[2]
    squared = jnp.zeros((own_coords.shape[1], width, part_coords.shape[2]), jnp.float32)
    for component in range(3):
        delta = own_coords[component][:, :, None] - part_coords[component][:, None, :]
        squared = squared + delta * delta
    scaled = decay_rate * jnp.sqrt(squared)
    kernel = variance * (1.0 + scaled) * jnp.exp(-scaled)
    column_pos = jnp.arange(part_coords.shape[2], dtype=jnp.int32) % width
    row_pos = jnp.arange(width, dtype=jnp.int32)
    same_leaf = jnp.repeat(part_ids == own_ids[:, None], width, axis=1)
    diagonal = same_leaf[:, None, :] & (column_pos[None, None, :] == row_pos[None, :, None])
    kernel = kernel + nugget * diagonal.astype(jnp.float32)
    live = jnp.repeat(present, width, axis=1).astype(jnp.float32)
    return (kernel * live[:, None, :]).astype(jnp.bfloat16)

def top_start(height, number):
    if height == 0:
        return 0
    return 2 * number - number // 2 ** (height - 1)

def reference(points, coords, basis, far_list, far_coupling, near_list, local_transfer, top_transfer, top_coupling):
    rhs_count = points.shape[0]
    leaf_total = LEAF_DEV * N_LEAF
    tree_bits = N_LEAF.bit_length() - 1
    basis_f = basis.reshape(leaf_total, LEAF, RANK).astype(jnp.float32)
    point_blocks = points.reshape(rhs_count, leaf_total, LEAF)
    leaf_coeff = jnp.einsum('lpk,rlp->lkr', basis_f, point_blocks.astype(jnp.float32), precision=highest).astype(jnp.bfloat16)

    def far_device(device_num):
        begin_leaf = device_num * LEAF_DEV
        partners = lax.dynamic_slice_in_dim(far_list, begin_leaf, LEAF_DEV, 0)
        coupling = lax.dynamic_slice_in_dim(far_coupling, begin_leaf, LEAF_DEV, 0).reshape(LEAF_DEV, NF, RANK, RANK)
        present = partners >= 0
        gathered = leaf_coeff[jnp.where(present, partners, 0)]
        gathered = jnp.where(present[:, :, None, None], gathered, jnp.zeros_like(gathered))
        return jnp.einsum('lsab,lsbr->lar', coupling.astype(jnp.float32), gathered.astype(jnp.float32), precision=highest)
    far_terms = lax.map(far_device, jnp.arange(N_LEAF, dtype=jnp.int32))
    transfer = local_transfer.reshape(N_LEAF, 2 * LEAF_DEV - 2, RANK, RANK).astype(jnp.float32)
    current = leaf_coeff.astype(jnp.float32).reshape(N_LEAF, LEAF_DEV, RANK, rhs_count)
    offset = 0
    number = LEAF_DEV
    matrices = []
    while number > 1:
        chosen = transfer[:, offset:offset + number]
        matrices.append(chosen)
        partial_value = jnp.einsum('dnab,dnar->dnbr', chosen, current, precision=highest)
        current = partial_value[:, 0::2] + partial_value[:, 1::2]
        offset += number
        number //= 2
    level_coeff = [current[:, 0]]
    for height in range(tree_bits - 2):
        number = N_LEAF >> height
        offset = top_start(height, N_LEAF)
        chosen = top_transfer[offset:offset + number].reshape(number, RANK, RANK).astype(jnp.float32)
        partial_value = jnp.einsum('nab,nar->nbr', chosen, level_coeff[height], precision=highest)
        level_coeff.append(partial_value[0::2] + partial_value[1::2])
    top_terms = []
    for height in range(tree_bits - 1):
        number = N_LEAF >> height
        offset = top_start(height, N_LEAF)
        coupling = top_coupling[offset:offset + number].reshape(number, 2, RANK, RANK).astype(jnp.float32)
        uncle = jnp.bitwise_xor(jnp.arange(number, dtype=jnp.int32) // 2, 1)
        cousin_left = level_coeff[height][2 * uncle]
        cousin_right = level_coeff[height][2 * uncle + 1]
        first_term = jnp.einsum('nab,nbr->nar', coupling[:, 0], cousin_left, precision=highest)
        second_term = jnp.einsum('nab,nbr->nar', coupling[:, 1], cousin_right, precision=highest)
        top_terms.append(first_term + second_term)
    field = top_terms[tree_bits - 2]
    for height in range(tree_bits - 2, 0, -1):
        number = N_LEAF >> height - 1
        offset = top_start(height - 1, N_LEAF)
        chosen = top_transfer[offset:offset + number].reshape(number, RANK, RANK).astype(jnp.float32)
        field = top_terms[height - 1] + jnp.einsum('nab,nbr->nar', chosen, jnp.repeat(field, 2, axis=0), precision=highest)
    field = field[:, None]
    for depth_num in range(len(matrices) - 1, -1, -1):
        spread = jnp.einsum('dnab,dnbr->dnar', matrices[depth_num], jnp.repeat(field, 2, axis=1), precision=highest)
        field = far_terms + spread if depth_num == 0 else spread
    leaf_field = field.reshape(leaf_total, RANK, rhs_count).astype(jnp.bfloat16)
    far_part = jnp.einsum('lpk,lkr->rlp', basis_f, leaf_field.astype(jnp.float32), precision=highest)
    far_part = far_part.reshape(rhs_count, leaf_total * LEAF)
    coord_blocks = coords.reshape(3, leaf_total, LEAF)
    block_leaves = min(16, LEAF_DEV)

    def near_block(block_num):
        begin_leaf = block_num * block_leaves
        own_ids = begin_leaf + jnp.arange(block_leaves, dtype=jnp.int32)
        partners = lax.dynamic_slice_in_dim(near_list, begin_leaf, block_leaves, 0)
        present = partners >= 0
        clamped = jnp.where(present, partners, own_ids[:, None])
        own_coords = lax.dynamic_slice_in_dim(coord_blocks, begin_leaf, block_leaves, 1)
        part_coords = coord_blocks[:, clamped].reshape(3, block_leaves, NN * LEAF)
        part_points = point_blocks[:, clamped].reshape(rhs_count, block_leaves, NN * LEAF)
        kernel = matern_block(own_coords, part_coords, own_ids, clamped, present)
        return jnp.einsum('bpq,rbq->rbp', kernel.astype(jnp.float32), part_points.astype(jnp.float32), precision=highest)
    near_part = lax.map(near_block, jnp.arange(leaf_total // block_leaves, dtype=jnp.int32))
    near_part = jnp.transpose(near_part, (1, 0, 2, 3)).reshape(rhs_count, leaf_total * LEAF)
    return near_part + far_part
```

```python
import functools
import math

import jax
import jax.numpy as jnp
from jax import lax
from jax.experimental import pallas as pl
from jax.experimental.pallas import tpu as pltpu
from jax.sharding import PartitionSpec as P

LEAF = 64
RANK = 32
NF = 16
NN = 12
SPAN = 8


variance = 1.0
nugget = 0.5
decay_rate = math.sqrt(3.0) / 0.3
highest = lax.Precision.HIGHEST


def padded(cells, sides, width):
    for axis, dim in sides:
        count = lax.axis_size(axis)
        ends = count - 1
        head = lax.slice_in_dim(cells, 0, width, axis=dim)
        tail = lax.slice_in_dim(cells, cells.shape[dim] - width, cells.shape[dim], axis=dim)
        cells = jnp.concatenate(
            [
                lax.ppermute(tail, axis, [(i, (i + 1) % count) for i in range(ends)]),
                cells,
                lax.ppermute(head, axis, [((i + 1) % count, i) for i in range(ends)]),
            ],
            axis=dim,
        )
    return cells


def swapped(block, axis, apart):
    count = lax.axis_size(axis)
    route = []
    for low in range(count):
        high = low | 1 << apart
        if high != low and high < count:
            route += [(low, high), (high, low)]
    return lax.ppermute(block, axis, route)


GROUP = 8


def near_kernel(leaves, empty, idx_ref, p_ref, qa_ref, qb_ref, x_ref, out_ref, acc, todo):
    def chunk(leaf, part):
        base = leaf * NN + part * 4
        j = [idx_ref[base + s] for s in range(4)]
        q = jnp.concatenate([qa_ref[j[0]] + qb_ref[j[1]], qa_ref[j[2]] + qb_ref[j[3]]], axis=1)
        t = jnp.dot(p_ref[leaf], q, preferred_element_type=jnp.float32)
        t = jnp.maximum(t, 1e-12)
        r = t * lax.rsqrt(t)
        k = ((1.0 + r) * jnp.exp(-r)).astype(jnp.bfloat16)
        x = jnp.concatenate([x_ref[j[s]] for s in range(4)], axis=0)
        return jnp.dot(k, x, preferred_element_type=jnp.float32)

    def first(g, carry):
        got = [chunk(g * GROUP + u, 0) for u in range(GROUP)]
        for u in range(GROUP):
            leaf = g * GROUP + u
            acc[leaf] = got[u] + nugget * x_ref[leaf + SPAN].astype(jnp.float32)
        return carry

    lax.fori_loop(0, leaves // GROUP, first, 0)

    def scan(leaf, n):
        for part in (1, 2):
            base = leaf * NN + part * 4
            low = idx_ref[base]
            for s in range(1, 4):
                low = jnp.minimum(low, idx_ref[base + s])
            todo[n] = leaf * 4 + part
            n = n + (low < empty).astype(jnp.int32)
        return n

    n = lax.fori_loop(0, leaves, scan, 0)
    for u in range(GROUP):
        todo[n + u] = leaves * 4

    def rest(g, carry):
        entries = [todo[g * GROUP + u] for u in range(GROUP)]
        got = [chunk(e // 4, e % 4) for e in entries]
        for u in range(GROUP):
            acc[entries[u] // 4] += got[u]
        return carry

    lax.fori_loop(0, (n + GROUP - 1) // GROUP, rest, 0)

    def turn(b, carry):
        block = acc[pl.ds(2 * b, 2)].reshape(2 * LEAF, x_ref.shape[2])
        out_ref[:, pl.ds(pl.multiple_of(b * 2 * LEAF, 2 * LEAF), 2 * LEAF)] = block.T
        return carry

    lax.fori_loop(0, leaves // 2, turn, 0)


def near_field(ext_points, ext_coords, near_list, device):
    rhs_count = ext_points.shape[0]
    leaves = near_list.shape[0]
    ext_leaves = leaves + 2 * SPAN
    own = slice(SPAN * LEAF, (SPAN + leaves) * LEAF)
    v = decay_rate * (ext_coords - ext_coords[:, SPAN * LEAF : SPAN * LEAF + 1])

    def split(f):
        h = lax.reduce_precision(f, 8, 7)
        m = lax.reduce_precision(f - h, 8, 7)
        return h, m, lax.reduce_precision(f - h - m, 8, 7)

    h, m, l = split(v)
    nh, nm, nl = split(jnp.sum(v * v, axis=0, keepdims=True))
    one = jnp.ones((3, v.shape[1]), jnp.float32)
    pad = jnp.zeros((8, v.shape[1]), jnp.float32)
    p = jnp.concatenate([h, h, m, m, h, l, nh, nm, nl, one, pad], 0)[:, own].astype(jnp.bfloat16)
    q = jnp.concatenate([h, m, h, m, l, h], 0) * -2.0
    q = jnp.concatenate([q, one, nh, nm, nl, pad], 0).astype(jnp.bfloat16)
    p = p.T.reshape(leaves, LEAF, 32)
    p = jnp.pad(p, ((0, 1), (0, 0), (0, 0)))
    q = q.reshape(32, ext_leaves, LEAF).transpose(1, 0, 2)
    qa = jnp.pad(q, ((0, 1), (0, 0), (0, LEAF)))
    qb = jnp.pad(q, ((0, 1), (0, 0), (LEAF, 0)))
    x = jnp.pad(ext_points.T.reshape(ext_leaves, LEAF, rhs_count), ((0, 1), (0, 0), (0, 0)))
    idx = jnp.where(near_list >= 0, near_list - device * leaves + SPAN, ext_leaves)
    idx = jnp.pad(idx, ((0, 1), (0, 0)), constant_values=ext_leaves).reshape(-1)
    vmem = pl.BlockSpec(memory_space=pltpu.VMEM)
    return pl.pallas_call(
        functools.partial(near_kernel, leaves, ext_leaves),
        out_shape=jax.ShapeDtypeStruct((rhs_count, leaves * LEAF), jnp.float32),
        in_specs=[pl.BlockSpec(memory_space=pltpu.SMEM)] + [vmem] * 4,
        out_specs=vmem,
        scratch_shapes=[
            pltpu.VMEM((leaves + 1, LEAF, rhs_count), jnp.float32),
            pltpu.SMEM((2 * leaves + GROUP + 8,), jnp.int32),
        ],
        compiler_params=pltpu.CompilerParams(vmem_limit_bytes=48 * 2**20),
        name="near",
    )(idx, p, qa, qb, x)


def top_start(height, number):
    if height == 0:
        return 0
    return 2 * number - number // 2 ** (height - 1)


def per_device(
    points,
    coords,
    basis,
    far_list,
    far_coupling,
    near_list,
    local_transfer,
    top_transfer,
    top_coupling,
):
    rhs_count = points.shape[0]
    leaf_local = basis.shape[0]
    device = lax.axis_index("leaf")
    devices_all = lax.axis_size("leaf")
    tree_bits = devices_all.bit_length() - 1
    basis_blocks = basis.reshape(leaf_local, LEAF, RANK)
    point_blocks = points.reshape(rhs_count, leaf_local, LEAF)
    leaf_coeff = jnp.einsum(
        "lpk,rlp->lkr", basis_blocks, point_blocks, preferred_element_type=jnp.float32
    ).astype(jnp.bfloat16)
    flat_coeff = leaf_coeff.reshape(leaf_local, RANK * rhs_count)
    ext_points = padded(points, (("leaf", 1),), SPAN * LEAF)
    ext_coords = padded(coords, (("leaf", 1),), SPAN * LEAF)
    present = far_list >= 0
    table = jnp.concatenate([flat_coeff] + [swapped(flat_coeff, "leaf", b) for b in range(tree_bits)], 0)
    apart = jnp.bitwise_xor(far_list // leaf_local, device)
    place = sum(jnp.where(apart == 1 << b, b + 1, 0) for b in range(tree_bits))
    row_index = jnp.where(present, place * leaf_local + far_list % leaf_local, 0)
    gathered = table[row_index]
    gathered = jnp.where(present[:, :, None], gathered, jnp.zeros_like(gathered))
    gathered = gathered.reshape(leaf_local, NF, RANK, rhs_count)
    coupling = far_coupling.reshape(leaf_local, NF, RANK, RANK)
    far_terms = jnp.einsum("lsab,lsbr->lar", coupling, gathered, preferred_element_type=jnp.float32)
    current = leaf_coeff.astype(jnp.float32)
    offset = 0
    number = leaf_local
    matrices = []
    while number > 1:
        chosen = (
            local_transfer[offset : offset + number].reshape(number, RANK, RANK).astype(jnp.float32)
        )
        matrices.append(chosen)
        partial_value = jnp.einsum("nab,nar->nbr", chosen, current, precision=highest)
        current = partial_value[0::2] + partial_value[1::2]
        offset += number
        number //= 2
    device_coeff = current[0]

    def top_matrix(height, node):
        picked = lax.dynamic_index_in_dim(
            top_transfer, top_start(height, devices_all) + node, 0, keepdims=False
        )
        return picked.reshape(RANK, RANK).astype(jnp.float32)

    top_terms = []
    mine = device_coeff
    before_mine = jnp.zeros_like(mine)
    before_sibling = jnp.zeros_like(mine)
    for height in range(tree_bits):
        received = swapped(jnp.stack([mine, before_mine, before_sibling]), "leaf", height)
        if height >= 1:
            lower = jnp.right_shift(device, height - 1)
            partner_first = lower % 2 == 0
            cousin_left = jnp.where(partner_first, received[1], received[2])
            cousin_right = jnp.where(partner_first, received[2], received[1])
            coupled_height = height - 1
            coupled_picked = lax.dynamic_index_in_dim(
                top_coupling, top_start(coupled_height, devices_all) + lower, 0, keepdims=False
            )
            pair = coupled_picked.reshape(2, RANK, RANK).astype(jnp.float32)
            top_terms.append(
                jnp.dot(pair[0], cousin_left, precision=highest)
                + jnp.dot(pair[1], cousin_right, precision=highest)
            )
        sibling = received[0]
        before_mine = mine
        before_sibling = sibling
        if height <= tree_bits - 3:
            node = jnp.right_shift(device, height)
            own_term = jnp.dot(top_matrix(height, node).T, mine, precision=highest)
            sibling_term = jnp.dot(
                top_matrix(height, jnp.bitwise_xor(node, 1)).T, sibling, precision=highest
            )
            mine = own_term + sibling_term
        else:
            mine = jnp.zeros_like(mine)
    field = top_terms[tree_bits - 2]
    for height in range(tree_bits - 2, 0, -1):
        child = jnp.right_shift(device, height - 1)
        field = top_terms[height - 1] + jnp.dot(
            top_matrix(height - 1, child), field, precision=highest
        )
    field = field[None]
    for depth_num in range(len(matrices) - 1, -1, -1):
        spread = jnp.einsum(
            "nab,nbr->nar", matrices[depth_num], jnp.repeat(field, 2, axis=0), precision=highest
        )
        field = far_terms + spread if depth_num == 0 else spread
    leaf_field = field.astype(jnp.bfloat16)
    far_part = jnp.einsum(
        "lpk,lkr->rlp", basis_blocks, leaf_field, preferred_element_type=jnp.float32
    )
    far_part = far_part.reshape(rhs_count, leaf_local * LEAF)
    near_part = near_field(ext_points, ext_coords, near_list, device)
    return near_part + far_part


def solution(mesh):
    return jax.shard_map(
        per_device,
        mesh=mesh,
        in_specs=(
            P(None, "leaf"),
            P(None, "leaf"),
            P("leaf", None),
            P("leaf", None),
            P("leaf", None, None),
            P("leaf", None),
            P("leaf", None),
            P(),
            P(),
        ),
        out_specs=P(None, "leaf"),
        check_vma=False,
    )
```

```python
import functools
import math

import jax
import jax.numpy as jnp
from jax import lax
from jax.experimental import pallas as pl
from jax.experimental.pallas import tpu as pltpu
from jax.sharding import PartitionSpec as P

LEAF = 64
RANK = 32
NF = 16
NN = 12
SPAN = 8
OCT = 8
HALO = SPAN * LEAF
GROUP = 8
MESH = pl.DeviceIdType.MESH

variance = 1.0
nugget = 0.5
decay_rate = math.sqrt(3.0) / 0.3
f32 = jnp.float32
bf16 = jnp.bfloat16


def top_start(height, number):
    if height == 0:
        return 0
    return 2 * number - number // 2 ** (height - 1)


def dot2(matrix, x):
    high = x.astype(bf16)
    low = (x - high.astype(f32)).astype(bf16)
    return jnp.dot(matrix, high, preferred_element_type=f32) + jnp.dot(
        matrix, low, preferred_element_type=f32
    )


def lane_group(rows, lanes, width):
    return lax.broadcasted_iota(jnp.int32, (rows, lanes), 1) // width


def pick(stacked, count, stride, rows, width):
    groups = lane_group(rows, stacked.shape[1], width)
    kept = jnp.zeros((rows, stacked.shape[1]), f32)
    for n in range(count):
        kept = jnp.where(groups == n * stride, stacked[n * rows : (n + 1) * rows], kept)
    return kept


def turned(x, shift):
    shift %= x.shape[1]
    return x if shift == 0 else pltpu.roll(x, shift, 1)


def up_kernel(rhs, octs, points_ref, basis_ref, up_ref, coeff_ref, top_ref):
    width = OCT * rhs
    row = lax.broadcasted_iota(jnp.int32, (width, OCT * LEAF), 0) // rhs
    own = row == lane_group(width, OCT * LEAF, LEAF)
    state = []
    for g in range(octs):
        cols = slice(g * OCT * LEAF, (g + 1) * OCT * LEAF)
        x = points_ref[:, cols].astype(f32)
        spread = jnp.where(own, jnp.concatenate([x] * OCT, 0), 0.0).astype(bf16)
        c = lax.dot_general(
            basis_ref[:, cols], spread, (((1,), (1,)), ((), ())), preferred_element_type=f32
        ).astype(bf16)
        coeff_ref[:, g * width : (g + 1) * width] = c
        state.append(c)
    offset = 0
    count = OCT
    while count >= 1:
        stride = OCT // count
        after = []
        for g in range(octs):
            rows = up_ref[(offset + g * count) * RANK : (offset + (g + 1) * count) * RANK]
            x = state[g]
            prod = jnp.dot(rows, x, preferred_element_type=f32) if count == OCT else dot2(rows, x)
            kept = pick(prod, count, stride, RANK, rhs)
            if count > 1:
                kept = kept + turned(kept, -stride * rhs)
            after.append(kept)
        state = after
        offset += octs * count
        count //= 2
    groups = lane_group(RANK, width, rhs)
    x = jnp.zeros((RANK, width), f32)
    for m in range(OCT):
        x = jnp.where(groups == m, turned(state[2 * m] + state[2 * m + 1], m * rhs), x)
    count = OCT
    while count > 1:
        stride = OCT // count
        rows = up_ref[offset * RANK : (offset + count) * RANK]
        kept = pick(dot2(rows, x), count, stride, RANK, rhs)
        x = kept + turned(kept, -stride * rhs)
        offset += count
        count //= 2
    small = lane_group(8, width, rhs)
    packed = jnp.zeros((8, width), f32)
    for m in range(RANK // 8):
        packed = jnp.where(small == m, turned(x[m * 8 : (m + 1) * 8], m * rhs), packed)
    top_ref[...] = packed


def spread_kernel(
    count, bits, coeff_ref, top_ref, points_ref, coords_ref,
    parts_ref, tops_ref, epoints_ref, ecoords_ref,
    send_sem, recv_sem, own_sem,
):
    me = lax.axis_index("leaf")
    size = points_ref.shape[1]

    def other(step):
        return lax.rem(me + step, count)

    def flipped(b):
        return me + (1 << b) - 2 * (1 << b) * (lax.div(me, 1 << b) % 2)

    barrier = pltpu.get_barrier_semaphore()

    def greet(step, carry):
        pl.semaphore_signal(barrier, inc=1, device_id=(other(step),), device_id_type=MESH)
        return carry

    lax.fori_loop(1, count, greet, 0)
    pl.semaphore_wait(barrier, count - 1)

    copies = []

    def send(src, dst, device):
        n = len(copies)
        copy = pltpu.make_async_remote_copy(
            src_ref=src, dst_ref=dst, send_sem=send_sem.at[n], recv_sem=recv_sem.at[n],
            device_id=(device,), device_id_type=MESH,
        )
        copy.start()
        copies.append(copy)

    for step in range(1, count):
        send(top_ref, tops_ref.at[step], other(step))
    left, right = other(count - 1), other(1)
    send(points_ref.at[:, pl.ds(size - HALO, HALO)], epoints_ref.at[:, pl.ds(0, HALO)], right)
    send(points_ref.at[:, pl.ds(0, HALO)], epoints_ref.at[:, pl.ds(HALO + size, HALO)], left)
    send(coords_ref.at[:, pl.ds(size - HALO, HALO)], ecoords_ref.at[:, pl.ds(0, HALO)], right)
    send(coords_ref.at[:, pl.ds(0, HALO)], ecoords_ref.at[:, pl.ds(HALO + size, HALO)], left)
    for b in reversed(range(bits)):
        send(coeff_ref, parts_ref.at[b + 1], flipped(b))
    own = [
        pltpu.make_async_copy(coeff_ref, parts_ref.at[0], own_sem.at[0]),
        pltpu.make_async_copy(top_ref, tops_ref.at[0], own_sem.at[1]),
        pltpu.make_async_copy(points_ref, epoints_ref.at[:, pl.ds(HALO, size)], own_sem.at[2]),
        pltpu.make_async_copy(coords_ref, ecoords_ref.at[:, pl.ds(HALO, size)], own_sem.at[3]),
    ]
    for copy in own:
        copy.start()
    for copy in own:
        copy.wait()
    for copy in copies:
        copy.wait()


def near_kernel(
    leaves, rhs, idx_ref, points_ref, coords_ref, out_ref, p_ref, qa_ref, qb_ref, x_ref, acc, todo
):
    empty = leaves + 2 * SPAN
    width = 2 * LEAF
    row = lax.broadcasted_iota(jnp.int32, (8, width), 0)
    low_half = lax.broadcasted_iota(jnp.int32, (48, width), 1) < LEAF
    origin = jnp.broadcast_to(coords_ref[:, HALO : HALO + width][:, :1], (8, width))

    def split(f):
        h = f.astype(bf16).astype(f32)
        m = (f - h).astype(bf16).astype(f32)
        return h, m, f - h - m

    def tables(b, own):
        cols = pl.ds(pl.multiple_of(b * width, width), width)
        v = jnp.where(row < 3, decay_rate * (coords_ref[:, cols] - origin), 0.0)
        norm = jnp.sum(v * v, axis=0, keepdims=True)
        one = jnp.ones_like(v)
        h, m, l = split(jnp.where(row < 3, -2.0 * v, jnp.where(row == 3, norm, jnp.where(row == 4, one, 0.0))))
        q = jnp.concatenate([h, m, h, m, l, h], 0)
        r = pltpu.roll(q, LEAF, 1)
        qa_ref[2 * b] = jnp.where(low_half, q, 0.0).astype(bf16)
        qb_ref[2 * b] = jnp.where(low_half, 0.0, r).astype(bf16)
        qa_ref[2 * b + 1] = jnp.where(low_half, r, 0.0).astype(bf16)
        qb_ref[2 * b + 1] = jnp.where(low_half, 0.0, q).astype(bf16)
        x = points_ref[:, cols].astype(f32).T.astype(bf16)
        x_ref[2 * b] = x[:LEAF]
        x_ref[2 * b + 1] = x[LEAF:]
        if own:
            h, m, l = split(jnp.where(row < 3, v, jnp.where(row == 3, one, jnp.where(row == 4, norm, 0.0))))
            p = jnp.concatenate([h, h, m, m, h, l], 0).T.astype(bf16)
            p_ref[2 * b - SPAN] = p[:LEAF]
            p_ref[2 * b + 1 - SPAN] = p[LEAF:]

    for b in range(SPAN // 2):
        tables(b, False)
        tables(b + (leaves + SPAN) // 2, False)
    lax.fori_loop(SPAN // 2, (leaves + SPAN) // 2, lambda b, c: (tables(b, True), c)[1], 0)
    qa_ref[empty] = jnp.zeros(qa_ref.shape[1:], bf16)
    qb_ref[empty] = jnp.zeros(qb_ref.shape[1:], bf16)
    x_ref[empty] = jnp.zeros(x_ref.shape[1:], bf16)
    p_ref[leaves] = jnp.zeros(p_ref.shape[1:], bf16)

    def chunk(leaf, part):
        base = leaf * NN + part * 4
        j = [idx_ref[base + s] for s in range(4)]
        q = jnp.concatenate([qa_ref[j[0]] + qb_ref[j[1]], qa_ref[j[2]] + qb_ref[j[3]]], axis=1)
        t = jnp.dot(p_ref[leaf], q, preferred_element_type=f32)
        t = jnp.maximum(t, 1e-12)
        r = t * lax.rsqrt(t)
        k = ((1.0 + r) * jnp.exp(-r)).astype(bf16)
        x = jnp.concatenate([x_ref[j[s]] for s in range(4)], axis=0)
        return jnp.dot(k, x, preferred_element_type=f32)

    def first(g, carry):
        got = [chunk(g * GROUP + u, 0) for u in range(GROUP)]
        for u in range(GROUP):
            leaf = g * GROUP + u
            acc[leaf] = got[u] + nugget * x_ref[leaf + SPAN].astype(f32)
        return carry

    lax.fori_loop(0, leaves // GROUP, first, 0)

    def scan(leaf, n):
        for part in (1, 2):
            base = leaf * NN + part * 4
            low = idx_ref[base]
            for s in range(1, 4):
                low = jnp.minimum(low, idx_ref[base + s])
            todo[n] = leaf * 4 + part
            n = n + (low < empty).astype(jnp.int32)
        return n

    n = lax.fori_loop(0, leaves, scan, 0)
    for u in range(GROUP):
        todo[n + u] = leaves * 4

    def rest(g, carry):
        entries = [todo[g * GROUP + u] for u in range(GROUP)]
        got = [chunk(lax.div(e, 4), lax.rem(e, 4)) for e in entries]
        for u in range(GROUP):
            acc[lax.div(entries[u], 4)] += got[u]
        return carry

    lax.fori_loop(0, lax.div(n + GROUP - 1, GROUP), rest, 0)

    def turn(b, carry):
        block = acc[pl.ds(2 * b, 2)].reshape(width, rhs)
        out_ref[:, pl.ds(pl.multiple_of(b * width, width), width)] = block.T
        return carry

    lax.fori_loop(0, leaves // 2, turn, 0)


def far_kernel(
    count, bits, rhs, octs, idx_ref, coupling_ref, parts_ref, tops_ref, pairs_ref, cousins_ref,
    steps_ref, down_ref, basis_ref, near_ref, out_ref, table, levels, fields, work, lined, far_at,
):
    g = pl.program_id(0)
    width = OCT * rhs
    leaves = octs * OCT
    groups = lane_group(RANK, width, rhs)

    @pl.when(g == 0)
    def _():
        device = lax.axis_index("leaf")
        source = lax.broadcasted_iota(jnp.int32, (width, OCT * width), 0)
        target = lax.broadcasted_iota(jnp.int32, (width, OCT * width), 1)
        repeat = (source == target // width * rhs + target % rhs).astype(f32).astype(bf16)

        def fill(block, carry):
            part = lax.div(block, octs)
            cols = pl.ds(pl.multiple_of(lax.rem(block, octs) * width, width), width)
            got = jnp.dot(parts_ref[part, :, cols], repeat, preferred_element_type=f32).astype(bf16)
            for n in range(OCT):
                table[block * OCT + n] = got[:, n * width : (n + 1) * width]
            return carry

        lax.fori_loop(0, (bits + 1) * octs, fill, 0)
        table[(bits + 1) * leaves] = jnp.zeros((RANK, width), bf16)

        def unpack(step, carry):
            packed = tops_ref[step]
            whole = jnp.concatenate([turned(packed, -m * rhs) for m in range(RANK // 8)], 0)
            levels[lax.rem(device - step + count, count)] = whole
            return carry

        lax.fori_loop(0, count, unpack, 0)
        number, base = count, 0
        for height in range(bits - 2):
            start = top_start(height, count) // 2
            for m in range(number // 2):
                both = jnp.concatenate([levels[base + 2 * m], levels[base + 2 * m + 1]], 0)
                levels[base + number + m] = dot2(pairs_ref[start + m], both)
            base += number
            number //= 2
        field = None
        for height in range(bits - 2, -1, -1):
            base = 2 * count - 2 * (count >> height)
            uncle = lax.rem(lax.div(device, 2 << height) + 1, 2) + 2 * lax.div(device, 4 << height)
            both = jnp.concatenate([levels[base + 2 * uncle], levels[base + 2 * uncle + 1]], 0)
            term = dot2(cousins_ref[height], both)
            field = term if field is None else term + dot2(steps_ref[height], field)
        x = jnp.where(groups == 0, field, 0.0)
        offset = 2 * leaves - 4
        cnt = 2
        while cnt <= OCT:
            stride = OCT // cnt
            x = x + turned(x, stride * rhs)
            rows = down_ref[offset * RANK : (offset + cnt) * RANK]
            x = pick(dot2(rows, x), cnt, stride, RANK, rhs)
            cnt *= 2
            offset -= cnt
        offset += cnt
        state = [jnp.where(groups == 0, turned(x, -(o // 2) * rhs), 0.0) for o in range(octs)]
        cnt = 1
        while cnt < OCT:
            stride = OCT // cnt
            offset -= octs * cnt
            after = []
            for o in range(octs):
                x = state[o]
                if cnt > 1:
                    x = x + turned(x, stride * rhs)
                rows = down_ref[(offset + o * cnt) * RANK : (offset + (o + 1) * cnt) * RANK]
                after.append(pick(dot2(rows, x), cnt, stride, RANK, rhs))
            state = after
            cnt *= 2
        for o in range(octs):
            fields[o] = state[o] + turned(state[o], rhs)

    weights = []
    masks = [(groups == n).astype(f32).astype(bf16) for n in range(OCT)]
    for s in range(NF):
        w = None
        for n in range(OCT):
            got = table[idx_ref[(g * OCT + n) * NF + s]] * masks[n]
            w = got if w is None else w + got
        weights.append(w)
    weights = jnp.concatenate(weights, 0)
    quarter = lane_group(8, 128, RANK)
    for n in range(OCT):
        c = coupling_ref[n].astype(f32)
        for t in range(8):
            work[n, pl.ds(t, NF, stride=8), :] = c[:, t * 128 : (t + 1) * 128]
        for q in range(NF // 4):
            v = [work[n, (q * 4 + s) * 8 : (q * 4 + s + 1) * 8, :] for s in range(4)]
            moved = []
            for a in range(4):
                y = turned(v[0], (0 - a) * RANK)
                for s in range(1, 4):
                    y = jnp.where(quarter == s, turned(v[s], (s - a) * RANK), y)
                moved.append(y)
            lined[n * RANK : (n + 1) * RANK, q * 128 : (q + 1) * 128] = jnp.concatenate(moved, 0).astype(bf16)
    far = pick(jnp.dot(lined[...], weights, preferred_element_type=f32), OCT, 1, RANK, rhs)
    for a in range(4):
        far_at[pl.ds(a, 8, stride=4), :] = far[a * 8 : (a + 1) * 8]
    rows = down_ref[pl.ds(pl.multiple_of(g * OCT * RANK, OCT * RANK), OCT * RANK), :]
    field = far_at[...] + pick(dot2(rows, fields[g]), OCT, 1, RANK, rhs)
    field = field.T.astype(bf16)
    got = jnp.dot(field, basis_ref[...], preferred_element_type=f32)
    out_ref[...] = near_ref[...] + pick(got, OCT, 1, rhs, LEAF)


def per_device(
    points, coords, basis, far_list, far_coupling, near_list, local_transfer, top_transfer, top_coupling
):
    rhs = points.shape[0]
    leaves = basis.shape[0]
    octs = leaves // OCT
    width = OCT * rhs
    size = leaves * LEAF
    device = lax.axis_index("leaf")
    count = lax.axis_size("leaf")
    bits = count.bit_length() - 1
    vmem = pl.BlockSpec(memory_space=pltpu.VMEM)
    smem = pl.BlockSpec(memory_space=pltpu.SMEM)
    limit = pltpu.CompilerParams(vmem_limit_bytes=48 * 2**20)

    basis_k = basis.reshape(leaves, LEAF, RANK).transpose(2, 0, 1).reshape(RANK, size)
    local = local_transfer.reshape(-1, RANK, RANK)
    down = local.reshape(-1, RANK)
    up = local.transpose(0, 2, 1).reshape(-1, RANK)
    coords8 = jnp.pad(coords, ((0, 5), (0, 0)))

    coeff, top = pl.pallas_call(
        functools.partial(up_kernel, rhs, octs),
        out_shape=(
            jax.ShapeDtypeStruct((RANK, leaves * rhs), bf16),
            jax.ShapeDtypeStruct((8, width), f32),
        ),
        in_specs=[vmem] * 3,
        out_specs=(vmem, vmem),
        compiler_params=limit,
        name="up",
    )(points, basis_k, up)

    total = count - 1 + 4 + bits
    parts, tops, ext_points, ext_coords = pl.pallas_call(
        functools.partial(spread_kernel, count, bits),
        out_shape=(
            jax.ShapeDtypeStruct((bits + 1, RANK, leaves * rhs), bf16),
            jax.ShapeDtypeStruct((count, 8, width), f32),
            jax.ShapeDtypeStruct((rhs, size + 2 * HALO), bf16),
            jax.ShapeDtypeStruct((8, size + 2 * HALO), f32),
        ),
        in_specs=[vmem] * 4,
        out_specs=(vmem,) * 4,
        scratch_shapes=[
            pltpu.SemaphoreType.DMA((total,)),
            pltpu.SemaphoreType.DMA((total,)),
            pltpu.SemaphoreType.DMA((4,)),
        ],
        compiler_params=pltpu.CompilerParams(
            vmem_limit_bytes=48 * 2**20, collective_id=0, has_side_effects=True
        ),
        name="spread",
    )(coeff, top, points, coords8)

    ext_leaves = leaves + 2 * SPAN
    near_idx = jnp.where(near_list >= 0, near_list - device * leaves + SPAN, ext_leaves)
    near_idx = jnp.pad(near_idx, ((0, 1), (0, 0)), constant_values=ext_leaves).reshape(-1)
    near_part = pl.pallas_call(
        functools.partial(near_kernel, leaves, rhs),
        out_shape=jax.ShapeDtypeStruct((rhs, size), f32),
        in_specs=[smem, vmem, vmem],
        out_specs=vmem,
        scratch_shapes=[
            pltpu.VMEM((leaves + 1, LEAF, 48), bf16),
            pltpu.VMEM((ext_leaves + 1, 48, 2 * LEAF), bf16),
            pltpu.VMEM((ext_leaves + 1, 48, 2 * LEAF), bf16),
            pltpu.VMEM((ext_leaves + 1, LEAF, rhs), bf16),
            pltpu.VMEM((leaves + 1, LEAF, rhs), f32),
            pltpu.SMEM((2 * leaves + GROUP + 8,), jnp.int32),
        ],
        compiler_params=limit,
        name="near",
    )(near_idx, ext_points, ext_coords)

    apart = jnp.bitwise_xor(far_list // leaves, device)
    place = sum(jnp.where(apart == 1 << b, b + 1, 0) for b in range(bits))
    far_idx = jnp.where(far_list >= 0, place * leaves + far_list % leaves, (bits + 1) * leaves).reshape(-1)
    pairs = top_transfer.reshape(-1, 2, RANK, RANK).transpose(0, 3, 1, 2).reshape(-1, RANK, 2 * RANK)
    rows = jnp.stack([top_start(h, count) + jnp.right_shift(device, h) for h in range(bits - 1)])
    cousins = top_coupling[rows].reshape(-1, 2, RANK, RANK).transpose(0, 2, 1, 3).reshape(-1, RANK, 2 * RANK)
    steps = top_transfer[rows].reshape(-1, RANK, RANK)
    whole = lambda *shape: pl.BlockSpec(shape, lambda g: (0,) * len(shape))
    return pl.pallas_call(
        functools.partial(far_kernel, count, bits, rhs, octs),
        grid=(octs,),
        out_shape=jax.ShapeDtypeStruct((rhs, size), f32),
        in_specs=[
            smem,
            pl.BlockSpec((OCT, NF, RANK * RANK), lambda g: (g, 0, 0)),
            whole(*parts.shape),
            whole(*tops.shape),
            whole(*pairs.shape),
            whole(*cousins.shape),
            whole(*steps.shape),
            whole(*down.shape),
            pl.BlockSpec((RANK, OCT * LEAF), lambda g: (0, g)),
            pl.BlockSpec((rhs, OCT * LEAF), lambda g: (0, g)),
        ],
        out_specs=pl.BlockSpec((rhs, OCT * LEAF), lambda g: (0, g)),
        scratch_shapes=[
            pltpu.VMEM(((bits + 1) * leaves + 1, RANK, width), bf16),
            pltpu.VMEM((2 * count, RANK, width), f32),
            pltpu.VMEM((octs, RANK, width), f32),
            pltpu.VMEM((OCT, 8 * NF, 128), f32),
            pltpu.VMEM((OCT * RANK, NF * RANK), bf16),
            pltpu.VMEM((RANK, width), f32),
        ],
        compiler_params=limit,
        name="far",
    )(far_idx, far_coupling, parts, tops, pairs, cousins, steps, down, basis_k, near_part)


def solution(mesh):
    return jax.shard_map(
        per_device,
        mesh=mesh,
        in_specs=(
            P(None, "leaf"),
            P(None, "leaf"),
            P("leaf", None),
            P("leaf", None),
            P("leaf", None, None),
            P("leaf", None),
            P("leaf", None),
            P(),
            P(),
        ),
        out_specs=P(None, "leaf"),
        check_vma=False,
    )
```

```python
import functools
import math

import jax
import jax.numpy as jnp
from jax import lax
from jax.experimental import pallas as pl
from jax.experimental.pallas import tpu as pltpu
from jax.sharding import PartitionSpec as P

LEAF = 64
RANK = 32
NF = 16
NN = 12
SPAN = 8
OCT = 8
HALO = SPAN * LEAF
GROUP = 8
EACH = 2
MESH = pl.DeviceIdType.MESH

variance = 1.0
nugget = 0.5
decay_rate = math.sqrt(3.0) / 0.3
f32 = jnp.float32
bf16 = jnp.bfloat16


def top_start(height, number):
    if height == 0:
        return 0
    return 2 * number - number // 2 ** (height - 1)


def halves(x):
    high = x.astype(bf16)
    return jnp.concatenate([high, (x - high.astype(f32)).astype(bf16)], 1)


def dot2(matrix, x, dims=((1,), (0,))):
    both = lax.dot_general(matrix, halves(x), (dims, ((), ())), preferred_element_type=f32)
    return both[:, : x.shape[1]] + both[:, x.shape[1] :]


def unfold(rows, work, out, base):
    tiles = rows.shape[1] // 128
    for t in range(tiles):
        work[pl.ds(t, 8, stride=tiles), :] = rows[:, t * 128 : (t + 1) * 128]
    for n in range(8 * tiles // 8):
        v = work[n * 8 : (n + 1) * 8, :]
        for q in range(4):
            out[pl.ds(base + n * 32 + q, 8, stride=4), :] = turned(v, -q * RANK)


def lane_group(rows, lanes, width):
    return lax.broadcasted_iota(jnp.int32, (rows, lanes), 1) // width


def pick(stacked, count, stride, rows, width):
    groups = lane_group(rows, stacked.shape[1], width)
    kept = jnp.zeros((rows, stacked.shape[1]), f32)
    for n in range(count):
        kept = jnp.where(groups == n * stride, stacked[n * rows : (n + 1) * rows], kept)
    return kept


def turned(x, shift):
    shift %= x.shape[1]
    return x if shift == 0 else pltpu.roll(x, shift, 1)


def up_kernel(
    rhs, octs, points_ref, basis_ref, local_ref, coeff_ref, top_ref, rows_ref, brows_ref,
    wide, spread_out, work, bwide, bout, bwork,
):
    width = OCT * rhs
    number = local_ref.shape[0]
    wide[0:number, :] = local_ref[...].astype(f32)
    bwide[...] = basis_ref[...].astype(f32)

    def open_local(block, carry):
        for u in range(2):
            rows = wide[pl.ds(pl.multiple_of((block * 2 + u) * 8, 8), 8), :]
            unfold(rows, work.at[u], spread_out.at[u], 0)
            at = pl.multiple_of((block * 2 + u) * 8 * RANK, 8 * RANK)
            rows_ref[pl.ds(at, 8 * RANK), :] = spread_out[u][:, :RANK].astype(bf16)
        return carry

    lax.fori_loop(0, wide.shape[0] // 16, open_local, 0)

    row = lax.broadcasted_iota(jnp.int32, (width, OCT * LEAF), 0) // rhs
    own = row == lane_group(width, OCT * LEAF, LEAF)
    state = []
    for g in range(octs):
        cols = slice(g * OCT * LEAF, (g + 1) * OCT * LEAF)
        unfold(bwide[g * OCT : (g + 1) * OCT, :], bwork.at[g % 2], bout.at[g % 2], 0)
        brows = bout[g % 2][:, :RANK].astype(bf16)
        brows_ref[cols, :] = brows
        x = points_ref[:, cols].astype(f32)
        spread = jnp.where(own, jnp.concatenate([x] * OCT, 0), 0.0).astype(bf16)
        c = jnp.dot(spread, brows, preferred_element_type=f32).T.astype(bf16)
        coeff_ref[:, g * width : (g + 1) * width] = c
        state.append(c.astype(f32))

    def apply(rows, x, count):
        mine = lax.broadcasted_iota(jnp.int32, (count * RANK, width), 0) // RANK * (OCT // count)
        tiled = jnp.where(mine == lane_group(count * RANK, width, rhs), jnp.concatenate([x] * count, 0), 0.0)
        return dot2(rows, tiled, ((0,), (0,)))

    offset = 0
    count = OCT
    while count >= 1:
        stride = OCT // count
        after = []
        for g in range(octs):
            rows = rows_ref[(offset + g * count) * RANK : (offset + (g + 1) * count) * RANK]
            kept = apply(rows, state[g], count)
            if count > 1:
                kept = kept + turned(kept, -stride * rhs)
            after.append(kept)
        state = after
        offset += octs * count
        count //= 2
    groups = lane_group(RANK, width, rhs)
    x = jnp.zeros((RANK, width), f32)
    for m in range(OCT):
        x = jnp.where(groups == m, turned(state[2 * m] + state[2 * m + 1], m * rhs), x)
    count = OCT
    while count > 1:
        stride = OCT // count
        rows = rows_ref[offset * RANK : (offset + count) * RANK]
        kept = apply(rows, x, count)
        x = kept + turned(kept, -stride * rhs)
        offset += count
        count //= 2
    small = lane_group(8, width, rhs)
    packed = jnp.zeros((8, width), f32)
    for m in range(RANK // 8):
        packed = jnp.where(small == m, turned(x[m * 8 : (m + 1) * 8], m * rhs), packed)
    top_ref[...] = packed


def spread_kernel(
    count, bits, coeff_ref, top_ref, points_ref, coords_ref,
    parts_ref, tops_ref, epoints_ref, ecoords_ref,
    send_sem, recv_sem, own_sem,
):
    me = lax.axis_index("leaf")
    size = points_ref.shape[1]

    def other(step):
        return lax.rem(me + step, count)

    def flipped(b):
        return me + (1 << b) - 2 * (1 << b) * (lax.div(me, 1 << b) % 2)

    barrier = pltpu.get_barrier_semaphore()

    def greet(step, carry):
        pl.semaphore_signal(barrier, inc=1, device_id=(other(step),), device_id_type=MESH)
        return carry

    lax.fori_loop(1, count, greet, 0)
    pl.semaphore_wait(barrier, count - 1)

    copies = []

    def send(src, dst, device):
        n = len(copies)
        copy = pltpu.make_async_remote_copy(
            src_ref=src, dst_ref=dst, send_sem=send_sem.at[n], recv_sem=recv_sem.at[n],
            device_id=(device,), device_id_type=MESH,
        )
        copy.start()
        copies.append(copy)

    for step in range(1, count):
        send(top_ref, tops_ref.at[step], other(step))
    left, right = other(count - 1), other(1)
    send(points_ref.at[:, pl.ds(size - HALO, HALO)], epoints_ref.at[:, pl.ds(0, HALO)], right)
    send(points_ref.at[:, pl.ds(0, HALO)], epoints_ref.at[:, pl.ds(HALO + size, HALO)], left)
    send(coords_ref.at[:, pl.ds(size - HALO, HALO)], ecoords_ref.at[:, pl.ds(0, HALO)], right)
    send(coords_ref.at[:, pl.ds(0, HALO)], ecoords_ref.at[:, pl.ds(HALO + size, HALO)], left)
    for b in reversed(range(bits)):
        send(coeff_ref, parts_ref.at[b + 1], flipped(b))
    own = [
        pltpu.make_async_copy(coeff_ref, parts_ref.at[0], own_sem.at[0]),
        pltpu.make_async_copy(top_ref, tops_ref.at[0], own_sem.at[1]),
        pltpu.make_async_copy(points_ref, epoints_ref.at[:, pl.ds(HALO, size)], own_sem.at[2]),
        pltpu.make_async_copy(coords_ref, ecoords_ref.at[:, pl.ds(HALO, size)], own_sem.at[3]),
    ]
    for copy in own:
        copy.start()
    for copy in own:
        copy.wait()
    for copy in copies:
        copy.wait()


def near_kernel(
    leaves, rhs, idx_ref, points_ref, coords_ref, out_ref, p_ref, qa_ref, qb_ref, x_ref, acc, todo
):
    empty = leaves + 2 * SPAN
    width = 2 * LEAF
    row = lax.broadcasted_iota(jnp.int32, (8, width), 0)
    low_half = lax.broadcasted_iota(jnp.int32, (48, width), 1) < LEAF
    origin = jnp.broadcast_to(coords_ref[:, HALO : HALO + width][:, :1], (8, width))

    def split(f):
        h = f.astype(bf16).astype(f32)
        m = (f - h).astype(bf16).astype(f32)
        return h, m, f - h - m

    def tables(b, own):
        cols = pl.ds(pl.multiple_of(b * width, width), width)
        v = jnp.where(row < 3, decay_rate * (coords_ref[:, cols] - origin), 0.0)
        norm = jnp.sum(v * v, axis=0, keepdims=True)
        one = jnp.ones_like(v)
        h, m, l = split(jnp.where(row < 3, -2.0 * v, jnp.where(row == 3, norm, jnp.where(row == 4, one, 0.0))))
        q = jnp.concatenate([h, m, h, m, l, h], 0)
        r = pltpu.roll(q, LEAF, 1)
        qa_ref[2 * b] = jnp.where(low_half, q, 0.0).astype(bf16)
        qb_ref[2 * b] = jnp.where(low_half, 0.0, r).astype(bf16)
        qa_ref[2 * b + 1] = jnp.where(low_half, r, 0.0).astype(bf16)
        qb_ref[2 * b + 1] = jnp.where(low_half, 0.0, q).astype(bf16)
        x = points_ref[:, cols].astype(f32).T.astype(bf16)
        x_ref[2 * b] = x[:LEAF]
        x_ref[2 * b + 1] = x[LEAF:]
        if own:
            h, m, l = split(jnp.where(row < 3, v, jnp.where(row == 3, one, jnp.where(row == 4, norm, 0.0))))
            p = jnp.concatenate([h, h, m, m, h, l], 0).T.astype(bf16)
            p_ref[2 * b - SPAN] = p[:LEAF]
            p_ref[2 * b + 1 - SPAN] = p[LEAF:]

    for b in range(SPAN // 2):
        tables(b, False)
        tables(b + (leaves + SPAN) // 2, False)

    def own_tables(g, carry):
        for u in range(GROUP):
            tables(SPAN // 2 + g * GROUP + u, True)
        return carry

    lax.fori_loop(0, leaves // 2 // GROUP, own_tables, 0)
    qa_ref[empty] = jnp.zeros(qa_ref.shape[1:], bf16)
    qb_ref[empty] = jnp.zeros(qb_ref.shape[1:], bf16)
    x_ref[empty] = jnp.zeros(x_ref.shape[1:], bf16)
    p_ref[leaves] = jnp.zeros(p_ref.shape[1:], bf16)

    def chunk(leaf, part):
        base = leaf * NN + part * 4
        j = [idx_ref[base + s] for s in range(4)]
        q = jnp.concatenate([qa_ref[j[0]] + qb_ref[j[1]], qa_ref[j[2]] + qb_ref[j[3]]], axis=1)
        t = jnp.dot(p_ref[leaf], q, preferred_element_type=f32)
        t = jnp.maximum(t, 1e-12)
        r = t * lax.rsqrt(t)
        k = ((1.0 + r) * jnp.exp(-r)).astype(bf16)
        x = jnp.concatenate([x_ref[j[s]] for s in range(4)], axis=0)
        return jnp.dot(k, x, preferred_element_type=f32)

    def first(g, carry):
        got = [chunk(g * GROUP + u, 0) for u in range(GROUP)]
        for u in range(GROUP):
            leaf = g * GROUP + u
            acc[leaf] = got[u] + nugget * x_ref[leaf + SPAN].astype(f32)
        return carry

    lax.fori_loop(0, leaves // GROUP, first, 0)

    def scan(g, n):
        for u in range(GROUP):
            leaf = g * GROUP + u
            for part in (1, 2):
                todo[n] = leaf * 4 + part
                n = n + idx_ref[(leaves + 1) * NN + leaf * 2 + part - 1]
        return n

    n = lax.fori_loop(0, leaves // GROUP, scan, 0)
    for u in range(GROUP):
        todo[n + u] = leaves * 4

    def rest(g, carry):
        entries = [todo[g * GROUP + u] for u in range(GROUP)]
        got = [chunk(lax.div(e, 4), lax.rem(e, 4)) for e in entries]
        for u in range(GROUP):
            acc[lax.div(entries[u], 4)] += got[u]
        return carry

    lax.fori_loop(0, lax.div(n + GROUP - 1, GROUP), rest, 0)

    def turn(g, carry):
        for u in range(GROUP):
            b = g * GROUP + u
            block = acc[pl.ds(2 * b, 2)].reshape(width, rhs)
            out_ref[:, pl.ds(pl.multiple_of(b * width, width), width)] = block.T
        return carry

    lax.fori_loop(0, leaves // 2 // GROUP, turn, 0)


def far_kernel(
    count, bits, rhs, octs, idx_ref, coupling_ref, parts_ref, tops_ref, transfer_ref, cousins_ref,
    down_ref, basis_ref, near_ref, out_ref, table, levels, fields, shift, lined, far_at,
    wide, top_rows, picked, cousin_rows, step_rows, work,
):
    g = pl.program_id(0)
    width = OCT * rhs
    leaves = octs * OCT
    groups = lane_group(RANK, width, rhs)

    @pl.when(g == 0)
    def _():
        device = lax.axis_index("leaf")
        source = lax.broadcasted_iota(jnp.int32, (width, OCT * width), 0)
        target = lax.broadcasted_iota(jnp.int32, (width, OCT * width), 1)
        repeat = (source == target // width * rhs + target % rhs).astype(f32).astype(bf16)

        def fill(part, carry):
            for o in range(octs):
                block = parts_ref[part, :, o * width : (o + 1) * width]
                got = jnp.dot(block, repeat, preferred_element_type=f32).astype(bf16)
                for n in range(OCT):
                    table[(part * octs + o) * OCT + n] = got[:, n * width : (n + 1) * width]
            return carry

        lax.fori_loop(0, bits + 1, fill, 0)
        table[(bits + 1) * leaves] = jnp.zeros((RANK, width), bf16)

        for step in range(count):
            packed = tops_ref[step]
            whole = jnp.concatenate([turned(packed, -m * rhs) for m in range(RANK // 8)], 0)
            levels[lax.rem(device - step + count, count)] = whole
        wide[0 : transfer_ref.shape[0], :] = transfer_ref[...].astype(f32)
        blocks = wide.shape[0] // 8
        for b in range(blocks):
            unfold(wide[b * 8 : (b + 1) * 8, :], work.at[b % OCT], top_rows, b * 8 * RANK)
        for height in range(bits - 1):
            at = top_start(height, count) + lax.div(device, 1 << height)
            picked[2 * height : 2 * height + 2, :] = cousins_ref[at].astype(f32)
            steps = top_rows[pl.ds(pl.multiple_of(at * RANK, RANK), RANK), :][:, :RANK]
            step_rows[height] = steps.astype(bf16)
        for b in range(picked.shape[0] // 8):
            unfold(picked[b * 8 : (b + 1) * 8, :], work.at[b % OCT], cousin_rows, b * 8 * RANK)
        number, base = count, 0
        for height in range(bits - 2):
            start = top_start(height, count)
            for m in range(number // 2):
                both = jnp.concatenate([levels[base + 2 * m], levels[base + 2 * m + 1]], 0)
                at = (start + 2 * m) * RANK
                two = top_rows[at : at + 2 * RANK, :][:, :RANK].astype(bf16)
                levels[base + number + m] = dot2(two, both, ((0,), (0,)))
            base += number
            number //= 2
        field = None
        for height in range(bits - 2, -1, -1):
            base = 2 * count - 2 * (count >> height)
            uncle = lax.rem(lax.div(device, 2 << height) + 1, 2) + 2 * lax.div(device, 4 << height)
            term = 0.0
            for side in range(2):
                at = (2 * height + side) * RANK
                matrix = cousin_rows[at : at + RANK, :][:, :RANK].astype(bf16)
                term = term + dot2(matrix, levels[base + 2 * uncle + side])
            field = term if field is None else term + dot2(step_rows[height], field)
        x = jnp.where(groups == 0, field, 0.0)
        offset = 2 * leaves - 4
        cnt = 2
        while cnt <= OCT:
            stride = OCT // cnt
            x = x + turned(x, stride * rhs)
            rows = down_ref[offset * RANK : (offset + cnt) * RANK]
            x = pick(dot2(rows, x), cnt, stride, RANK, rhs)
            cnt *= 2
            offset -= cnt
        offset += cnt
        state = [jnp.where(groups == 0, turned(x, -(o // 2) * rhs), 0.0) for o in range(octs)]
        cnt = 1
        while cnt < OCT:
            stride = OCT // cnt
            offset -= octs * cnt
            after = []
            for o in range(octs):
                x = state[o]
                if cnt > 1:
                    x = x + turned(x, stride * rhs)
                rows = down_ref[(offset + o * cnt) * RANK : (offset + (o + 1) * cnt) * RANK]
                after.append(pick(dot2(rows, x), cnt, stride, RANK, rhs))
            state = after
            cnt *= 2
        for o in range(octs):
            fields[o] = state[o] + turned(state[o], rhs)

    for u in range(EACH):
        o = g * EACH + u
        weights = []
        masks = [(groups == n).astype(f32).astype(bf16) for n in range(OCT)]
        for s in range(NF):
            w = None
            for n in range(OCT):
                got = table[idx_ref[(o * OCT + n) * NF + s]] * masks[n]
                w = got if w is None else w + got
            weights.append(w)
        weights = jnp.concatenate(weights, 0)
        quarter = lane_group(8, 128, RANK)
        for n in range(OCT):
            c = coupling_ref[u * OCT + n].astype(f32)
            for t in range(8):
                shift[u, n, pl.ds(t, NF, stride=8), :] = c[:, t * 128 : (t + 1) * 128]
            for q in range(NF // 4):
                v = [shift[u, n, (q * 4 + s) * 8 : (q * 4 + s + 1) * 8, :] for s in range(4)]
                moved = []
                for a in range(4):
                    y = turned(v[0], (0 - a) * RANK)
                    for s in range(1, 4):
                        y = jnp.where(quarter == s, turned(v[s], (s - a) * RANK), y)
                    moved.append(y)
                lined[u, n * RANK : (n + 1) * RANK, q * 128 : (q + 1) * 128] = jnp.concatenate(moved, 0).astype(bf16)
        far = pick(jnp.dot(lined[u], weights, preferred_element_type=f32), OCT, 1, RANK, rhs)
        for a in range(4):
            far_at[u, pl.ds(a, 8, stride=4), :] = far[a * 8 : (a + 1) * 8]
        rows = down_ref[pl.ds(pl.multiple_of(o * OCT * RANK, OCT * RANK), OCT * RANK), :]
        field = far_at[u] + pick(dot2(rows, fields[o]), OCT, 1, RANK, rhs)
        field = field.T.astype(bf16)
        cols = slice(u * OCT * LEAF, (u + 1) * OCT * LEAF)
        got = lax.dot_general(field, basis_ref[cols, :], (((1,), (1,)), ((), ())), preferred_element_type=f32)
        out_ref[:, cols] = near_ref[:, cols] + pick(got, OCT, 1, rhs, LEAF)


def per_device(
    points, coords, basis, far_list, far_coupling, near_list, local_transfer, top_transfer, top_coupling
):
    rhs = points.shape[0]
    leaves = basis.shape[0]
    octs = leaves // OCT
    width = OCT * rhs
    size = leaves * LEAF
    device = lax.axis_index("leaf")
    count = lax.axis_size("leaf")
    bits = count.bit_length() - 1
    vmem = pl.BlockSpec(memory_space=pltpu.VMEM)
    smem = pl.BlockSpec(memory_space=pltpu.SMEM)
    limit = pltpu.CompilerParams(vmem_limit_bytes=48 * 2**20)

    def room(n):
        return -(-n // 16) * 16

    nodes = room(local_transfer.shape[0])
    coords8 = jnp.pad(coords, ((0, 5), (0, 0)))

    coeff, top, down, brows = pl.pallas_call(
        functools.partial(up_kernel, rhs, octs),
        out_shape=(
            jax.ShapeDtypeStruct((RANK, leaves * rhs), bf16),
            jax.ShapeDtypeStruct((8, width), f32),
            jax.ShapeDtypeStruct((nodes * RANK, RANK), bf16),
            jax.ShapeDtypeStruct((size, RANK), bf16),
        ),
        in_specs=[vmem] * 3,
        out_specs=(vmem,) * 4,
        scratch_shapes=[
            pltpu.VMEM((nodes, RANK * RANK), f32),
            pltpu.VMEM((2, 8 * RANK, 128), f32),
            pltpu.VMEM((2, 64, 128), f32),
            pltpu.VMEM((leaves, LEAF * RANK), f32),
            pltpu.VMEM((2, OCT * LEAF, 128), f32),
            pltpu.VMEM((2, 128, 128), f32),
        ],
        compiler_params=limit,
        name="up",
    )(points, basis, local_transfer)

    total = count - 1 + 4 + bits
    parts, tops, ext_points, ext_coords = pl.pallas_call(
        functools.partial(spread_kernel, count, bits),
        out_shape=(
            jax.ShapeDtypeStruct((bits + 1, RANK, leaves * rhs), bf16),
            jax.ShapeDtypeStruct((count, 8, width), f32),
            jax.ShapeDtypeStruct((rhs, size + 2 * HALO), bf16),
            jax.ShapeDtypeStruct((8, size + 2 * HALO), f32),
        ),
        in_specs=[vmem] * 4,
        out_specs=(vmem,) * 4,
        scratch_shapes=[
            pltpu.SemaphoreType.DMA((total,)),
            pltpu.SemaphoreType.DMA((total,)),
            pltpu.SemaphoreType.DMA((4,)),
        ],
        compiler_params=pltpu.CompilerParams(
            vmem_limit_bytes=48 * 2**20, collective_id=0, has_side_effects=True
        ),
        name="spread",
    )(coeff, top, points, coords8)

    ext_leaves = leaves + 2 * SPAN
    near_idx = jnp.where(near_list >= 0, near_list - device * leaves + SPAN, ext_leaves)
    used = (jnp.max(near_list[:, 4:].reshape(leaves, 2, 4), axis=2) >= 0).astype(jnp.int32)
    near_idx = jnp.pad(near_idx, ((0, 1), (0, 0)), constant_values=ext_leaves).reshape(-1)
    near_idx = jnp.concatenate([near_idx, used.reshape(-1)])
    near_part = pl.pallas_call(
        functools.partial(near_kernel, leaves, rhs),
        out_shape=jax.ShapeDtypeStruct((rhs, size), f32),
        in_specs=[smem, vmem, vmem],
        out_specs=vmem,
        scratch_shapes=[
            pltpu.VMEM((leaves + 1, LEAF, 48), bf16),
            pltpu.VMEM((ext_leaves + 1, 48, 2 * LEAF), bf16),
            pltpu.VMEM((ext_leaves + 1, 48, 2 * LEAF), bf16),
            pltpu.VMEM((ext_leaves + 1, LEAF, rhs), bf16),
            pltpu.VMEM((leaves + 1, LEAF, rhs), f32),
            pltpu.SMEM((2 * leaves + GROUP + 8,), jnp.int32),
        ],
        compiler_params=limit,
        name="near",
    )(near_idx, ext_points, ext_coords)

    apart = jnp.bitwise_xor(far_list // leaves, device)
    place = sum(jnp.where(apart == 1 << b, b + 1, 0) for b in range(bits))
    far_idx = jnp.where(far_list >= 0, place * leaves + far_list % leaves, (bits + 1) * leaves).reshape(-1)
    whole = lambda *shape: pl.BlockSpec(shape, lambda g: (0,) * len(shape))
    return pl.pallas_call(
        functools.partial(far_kernel, count, bits, rhs, octs),
        grid=(octs // EACH,),
        out_shape=jax.ShapeDtypeStruct((rhs, size), f32),
        in_specs=[
            smem,
            pl.BlockSpec((EACH * OCT, NF, RANK * RANK), lambda g: (g, 0, 0)),
            whole(*parts.shape),
            whole(*tops.shape),
            whole(*top_transfer.shape),
            whole(*top_coupling.shape),
            whole(*down.shape),
            pl.BlockSpec((EACH * OCT * LEAF, RANK), lambda g: (g, 0)),
            pl.BlockSpec((rhs, EACH * OCT * LEAF), lambda g: (0, g)),
        ],
        out_specs=pl.BlockSpec((rhs, EACH * OCT * LEAF), lambda g: (0, g)),
        scratch_shapes=[
            pltpu.VMEM(((bits + 1) * leaves + 1, RANK, width), bf16),
            pltpu.VMEM((2 * count, RANK, width), f32),
            pltpu.VMEM((octs, RANK, width), f32),
            pltpu.VMEM((EACH, OCT, 8 * NF, 128), f32),
            pltpu.VMEM((EACH, OCT * RANK, NF * RANK), bf16),
            pltpu.VMEM((EACH, RANK, width), f32),
            pltpu.VMEM((room(top_transfer.shape[0]), RANK * RANK), f32),
            pltpu.VMEM((room(top_transfer.shape[0]) * RANK, 128), f32),
            pltpu.VMEM((room(2 * bits), RANK * RANK), f32),
            pltpu.VMEM((room(2 * bits) * RANK, 128), f32),
            pltpu.VMEM((bits, RANK, RANK), bf16),
            pltpu.VMEM((OCT, 64, 128), f32),
        ],
        compiler_params=limit,
        name="far",
    )(far_idx, far_coupling, parts, tops, top_transfer, top_coupling, down, brows, near_part)


def solution(mesh):
    return jax.shard_map(
        per_device,
        mesh=mesh,
        in_specs=(
            P(None, "leaf"),
            P(None, "leaf"),
            P("leaf", None),
            P("leaf", None),
            P("leaf", None, None),
            P("leaf", None),
            P("leaf", None),
            P(),
            P(),
        ),
        out_specs=P(None, "leaf"),
        check_vma=False,
    )
```

```python
import functools
import math

import jax
import jax.numpy as jnp
from jax import lax
from jax.experimental import pallas as pl
from jax.experimental.pallas import tpu as pltpu
from jax.sharding import PartitionSpec as P

LEAF = 64
RANK = 32
NF = 16
NN = 12
SPAN = 8
OCT = 8
HALO = SPAN * LEAF
GROUP = 8
EACH = 2
MESH = pl.DeviceIdType.MESH

variance = 1.0
nugget = 0.5
decay_rate = math.sqrt(3.0) / 0.3
f32 = jnp.float32
bf16 = jnp.bfloat16


def top_start(height, number):
    if height == 0:
        return 0
    return 2 * number - number // 2 ** (height - 1)


def halves(x):
    high = x.astype(bf16)
    return jnp.concatenate([high, (x - high.astype(f32)).astype(bf16)], 1)


def dot2(matrix, x, dims=((1,), (0,))):
    both = lax.dot_general(matrix, halves(x), (dims, ((), ())), preferred_element_type=f32)
    return both[:, : x.shape[1]] + both[:, x.shape[1] :]


def unfold(rows, work, out, base):
    tiles = rows.shape[1] // 128
    for t in range(tiles):
        work[pl.ds(t, 8, stride=tiles), :] = rows[:, t * 128 : (t + 1) * 128]
    for n in range(8 * tiles // 8):
        v = work[n * 8 : (n + 1) * 8, :]
        for q in range(4):
            out[pl.ds(base + n * 32 + q, 8, stride=4), :] = turned(v, -q * RANK)


def lane_group(rows, lanes, width):
    return lax.broadcasted_iota(jnp.int32, (rows, lanes), 1) // width


def pick(stacked, count, stride, rows, width):
    groups = lane_group(rows, stacked.shape[1], width)
    kept = jnp.zeros((rows, stacked.shape[1]), f32)
    for n in range(count):
        kept = jnp.where(groups == n * stride, stacked[n * rows : (n + 1) * rows], kept)
    return kept


def turned(x, shift):
    shift %= x.shape[1]
    return x if shift == 0 else pltpu.roll(x, shift, 1)


def up_kernel(
    rhs, octs, points_ref, basis_ref, local_ref, coeff_ref, top_ref, rows_ref, brows_ref,
    wide, spread_out, work, bwide, bout, bwork,
):
    width = OCT * rhs
    number = local_ref.shape[0]
    wide[0:number, :] = local_ref[...].astype(f32)
    bwide[...] = basis_ref[...].astype(f32)

    def open_local(block, carry):
        for u in range(2):
            rows = wide[pl.ds(pl.multiple_of((block * 2 + u) * 8, 8), 8), :]
            unfold(rows, work.at[u], spread_out.at[u], 0)
            at = pl.multiple_of((block * 2 + u) * 8 * RANK, 8 * RANK)
            rows_ref[pl.ds(at, 8 * RANK), :] = spread_out[u][:, :RANK].astype(bf16)
        return carry

    lax.fori_loop(0, wide.shape[0] // 16, open_local, 0)

    row = lax.broadcasted_iota(jnp.int32, (width, OCT * LEAF), 0) // rhs
    own = row == lane_group(width, OCT * LEAF, LEAF)
    state = []
    for g in range(octs):
        cols = slice(g * OCT * LEAF, (g + 1) * OCT * LEAF)
        unfold(bwide[g * OCT : (g + 1) * OCT, :], bwork.at[g % 2], bout.at[g % 2], 0)
        brows = bout[g % 2][:, :RANK].astype(bf16)
        brows_ref[cols, :] = brows
        x = points_ref[:, cols].astype(f32)
        spread = jnp.where(own, jnp.concatenate([x] * OCT, 0), 0.0).astype(bf16)
        c = jnp.dot(spread, brows, preferred_element_type=f32).T.astype(bf16)
        coeff_ref[:, g * width : (g + 1) * width] = c
        state.append(c.astype(f32))

    def apply(rows, x, count):
        mine = lax.broadcasted_iota(jnp.int32, (count * RANK, width), 0) // RANK * (OCT // count)
        tiled = jnp.where(mine == lane_group(count * RANK, width, rhs), jnp.concatenate([x] * count, 0), 0.0)
        return dot2(rows, tiled, ((0,), (0,)))

    offset = 0
    count = OCT
    while count >= 1:
        stride = OCT // count
        after = []
        for g in range(octs):
            rows = rows_ref[(offset + g * count) * RANK : (offset + (g + 1) * count) * RANK]
            kept = apply(rows, state[g], count)
            if count > 1:
                kept = kept + turned(kept, -stride * rhs)
            after.append(kept)
        state = after
        offset += octs * count
        count //= 2
    groups = lane_group(RANK, width, rhs)
    x = jnp.zeros((RANK, width), f32)
    for m in range(OCT):
        x = jnp.where(groups == m, turned(state[2 * m] + state[2 * m + 1], m * rhs), x)
    count = OCT
    while count > 1:
        stride = OCT // count
        rows = rows_ref[offset * RANK : (offset + count) * RANK]
        kept = apply(rows, x, count)
        x = kept + turned(kept, -stride * rhs)
        offset += count
        count //= 2
    small = lane_group(8, width, rhs)
    packed = jnp.zeros((8, width), f32)
    for m in range(RANK // 8):
        packed = jnp.where(small == m, turned(x[m * 8 : (m + 1) * 8], m * rhs), packed)
    top_ref[...] = packed


def near_kernel(
    count, bits, leaves, rhs, list_ref, coeff_ref, top_ref, points_ref, coords_ref,
    parts_ref, tops_ref, out_ref,
    wide, halo_points, halo_coords, p_ref, qa_ref, qb_ref, x_ref, acc, send_sem, recv_sem, own_sem,
):
    me = lax.axis_index("leaf")
    size = points_ref.shape[1]

    def other(step):
        return lax.rem(me + step, count)

    def flipped(b):
        return me + (1 << b) - 2 * (1 << b) * lax.rem(lax.div(me, 1 << b), 2)

    barrier = pltpu.get_barrier_semaphore()

    def greet(step, carry):
        pl.semaphore_signal(barrier, inc=1, device_id=(other(step),), device_id_type=MESH)
        return carry

    lax.fori_loop(1, count, greet, 0)
    wide[0:3, :] = coords_ref[...]
    wide[3:8, :] = jnp.zeros((5, size), f32)
    pl.semaphore_wait(barrier, count - 1)

    copies = []

    def send(src, dst, device):
        n = len(copies)
        copy = pltpu.make_async_remote_copy(
            src_ref=src, dst_ref=dst, send_sem=send_sem.at[n], recv_sem=recv_sem.at[n],
            device_id=(device,), device_id_type=MESH,
        )
        copy.start()
        copies.append(copy)

    left, right = other(count - 1), other(1)
    send(points_ref.at[:, pl.ds(size - HALO, HALO)], halo_points.at[0], right)
    send(points_ref.at[:, pl.ds(0, HALO)], halo_points.at[1], left)
    send(wide.at[:, pl.ds(size - HALO, HALO)], halo_coords.at[0], right)
    send(wide.at[:, pl.ds(0, HALO)], halo_coords.at[1], left)
    for b in reversed(range(bits)):
        send(coeff_ref, parts_ref.at[b + 1], flipped(b))
    for step in range(1, count):
        send(top_ref, tops_ref.at[step], other(step))
    own_copies = [
        pltpu.make_async_copy(coeff_ref, parts_ref.at[0], own_sem.at[0]),
        pltpu.make_async_copy(top_ref, tops_ref.at[0], own_sem.at[1]),
    ]
    for copy in own_copies:
        copy.start()

    empty = leaves + 2 * SPAN
    width = 2 * LEAF
    row = lax.broadcasted_iota(jnp.int32, (8, width), 0)
    low_half = lax.broadcasted_iota(jnp.int32, (48, width), 1) < LEAF
    origin = jnp.broadcast_to(wide[:, 0:width][:, :1], (8, width))

    def split(f):
        h = f.astype(bf16).astype(f32)
        m = (f - h).astype(bf16).astype(f32)
        return h, m, f - h - m

    def tables(b, own, pts, xyz):
        v = jnp.where(row < 3, decay_rate * (xyz - origin), 0.0)
        norm = jnp.sum(v * v, axis=0, keepdims=True)
        one = jnp.ones_like(v)
        h, m, l = split(jnp.where(row < 3, -2.0 * v, jnp.where(row == 3, norm, jnp.where(row == 4, one, 0.0))))
        q = jnp.concatenate([h, m, h, m, l, h], 0)
        r = pltpu.roll(q, LEAF, 1)
        qa_ref[2 * b] = jnp.where(low_half, q, 0.0).astype(bf16)
        qb_ref[2 * b] = jnp.where(low_half, 0.0, r).astype(bf16)
        qa_ref[2 * b + 1] = jnp.where(low_half, r, 0.0).astype(bf16)
        qb_ref[2 * b + 1] = jnp.where(low_half, 0.0, q).astype(bf16)
        x = pts.astype(f32).T.astype(bf16)
        x_ref[2 * b] = x[:LEAF]
        x_ref[2 * b + 1] = x[LEAF:]
        if own:
            h, m, l = split(jnp.where(row < 3, v, jnp.where(row == 3, one, jnp.where(row == 4, norm, 0.0))))
            p = jnp.concatenate([h, h, m, m, h, l], 0).T.astype(bf16)
            p_ref[2 * b - SPAN] = p[:LEAF]
            p_ref[2 * b + 1 - SPAN] = p[LEAF:]

    qa_ref[empty] = jnp.zeros(qa_ref.shape[1:], bf16)
    qb_ref[empty] = jnp.zeros(qb_ref.shape[1:], bf16)
    x_ref[empty] = jnp.zeros(x_ref.shape[1:], bf16)

    def own_tables(g, carry):
        for u in range(GROUP):
            b = g * GROUP + u
            cols = pl.ds(pl.multiple_of(b * width, width), width)
            tables(SPAN // 2 + b, True, points_ref[:, cols], wide[:, cols])
        return carry

    lax.fori_loop(0, leaves // 2 // GROUP, own_tables, 0)
    base = me * leaves - SPAN

    def leaf_product(leaf):
        t = []
        x = []
        for part in range(NN // 4):
            j = []
            for s in range(4):
                entry = list_ref[leaf, part * 4 + s]
                j.append(jnp.where(entry >= 0, jnp.clip(entry - base, 0, empty), empty))
                x.append(x_ref[j[s]])
            q = jnp.concatenate([qa_ref[j[0]] + qb_ref[j[1]], qa_ref[j[2]] + qb_ref[j[3]]], axis=1)
            v = jnp.dot(p_ref[leaf], q, preferred_element_type=f32)
            v = jnp.maximum(v, 1e-12)
            r = v * lax.rsqrt(v)
            t.append(((1.0 + r) * jnp.exp(-r)).astype(bf16))
        return jnp.dot(jnp.concatenate(t, 1), jnp.concatenate(x, 0), preferred_element_type=f32)

    def group(g, carry):
        got = [leaf_product(g * GROUP + u) for u in range(GROUP)]
        for u in range(GROUP):
            leaf = g * GROUP + u
            acc[leaf] = got[u] + nugget * x_ref[leaf + SPAN].astype(f32)
        return carry

    lax.fori_loop(SPAN // GROUP, (leaves - SPAN) // GROUP, group, 0)
    for n in range(4):
        copies[n].wait()
    for side in range(2):
        for b in range(SPAN // 2):
            cols = slice(b * width, (b + 1) * width)
            at = b + side * (leaves + SPAN) // 2
            tables(at, False, halo_points[side, :, cols], halo_coords[side, :, cols])
    lax.fori_loop(0, SPAN // GROUP, group, 0)
    lax.fori_loop((leaves - SPAN) // GROUP, leaves // GROUP, group, 0)

    def turn(g, carry):
        for u in range(GROUP):
            b = g * GROUP + u
            block = acc[pl.ds(2 * b, 2)].reshape(width, rhs)
            out_ref[:, pl.ds(pl.multiple_of(b * width, width), width)] = block.T
        return carry

    lax.fori_loop(0, leaves // 2 // GROUP, turn, 0)
    for copy in own_copies:
        copy.wait()
    for copy in copies[4:]:
        copy.wait()


def far_kernel(
    count, bits, rhs, octs, idx_ref, coupling_ref, parts_ref, tops_ref, transfer_ref, cousins_ref,
    down_ref, basis_ref, near_ref, out_ref, table, levels, fields, shift, lined, far_at,
    wide, top_rows, picked, cousin_rows, step_rows, work, lut,
):
    g = pl.program_id(0)
    width = OCT * rhs
    leaves = octs * OCT
    groups = lane_group(RANK, width, rhs)

    @pl.when(g == 0)
    def _():
        device = lax.axis_index("leaf")
        lut[0] = (bits + 1) * leaves - (leaves - 1)
        lut[device + 1] = 0
        for b in range(bits):
            lut[jnp.bitwise_xor(device, 1 << b) + 1] = (b + 1) * leaves
        source = lax.broadcasted_iota(jnp.int32, (width, OCT * width), 0)
        target = lax.broadcasted_iota(jnp.int32, (width, OCT * width), 1)
        repeat = (source == target // width * rhs + target % rhs).astype(f32).astype(bf16)

        def fill(part, carry):
            for o in range(octs):
                block = parts_ref[part, :, o * width : (o + 1) * width]
                got = jnp.dot(block, repeat, preferred_element_type=f32).astype(bf16)
                for n in range(OCT):
                    table[(part * octs + o) * OCT + n] = got[:, n * width : (n + 1) * width]
            return carry

        lax.fori_loop(0, bits + 1, fill, 0)
        table[(bits + 1) * leaves] = jnp.zeros((RANK, width), bf16)

        for step in range(count):
            packed = tops_ref[step]
            whole = jnp.concatenate([turned(packed, -m * rhs) for m in range(RANK // 8)], 0)
            levels[lax.rem(device - step + count, count)] = whole
        wide[0 : transfer_ref.shape[0], :] = transfer_ref[...].astype(f32)
        blocks = wide.shape[0] // 8
        for b in range(blocks):
            unfold(wide[b * 8 : (b + 1) * 8, :], work.at[b % OCT], top_rows, b * 8 * RANK)
        for height in range(bits - 1):
            at = top_start(height, count) + lax.div(device, 1 << height)
            picked[2 * height : 2 * height + 2, :] = cousins_ref[at].astype(f32)
            steps = top_rows[pl.ds(pl.multiple_of(at * RANK, RANK), RANK), :][:, :RANK]
            step_rows[height] = steps.astype(bf16)
        for b in range(picked.shape[0] // 8):
            unfold(picked[b * 8 : (b + 1) * 8, :], work.at[b % OCT], cousin_rows, b * 8 * RANK)
        number, base = count, 0
        for height in range(bits - 2):
            start = top_start(height, count)
            for m in range(number // 2):
                both = jnp.concatenate([levels[base + 2 * m], levels[base + 2 * m + 1]], 0)
                at = (start + 2 * m) * RANK
                two = top_rows[at : at + 2 * RANK, :][:, :RANK].astype(bf16)
                levels[base + number + m] = dot2(two, both, ((0,), (0,)))
            base += number
            number //= 2
        field = None
        for height in range(bits - 2, -1, -1):
            base = 2 * count - 2 * (count >> height)
            uncle = lax.rem(lax.div(device, 2 << height) + 1, 2) + 2 * lax.div(device, 4 << height)
            term = 0.0
            for side in range(2):
                at = (2 * height + side) * RANK
                matrix = cousin_rows[at : at + RANK, :][:, :RANK].astype(bf16)
                term = term + dot2(matrix, levels[base + 2 * uncle + side])
            field = term if field is None else term + dot2(step_rows[height], field)
        x = jnp.where(groups == 0, field, 0.0)
        offset = 2 * leaves - 4
        cnt = 2
        while cnt <= OCT:
            stride = OCT // cnt
            x = x + turned(x, stride * rhs)
            rows = down_ref[offset * RANK : (offset + cnt) * RANK]
            x = pick(dot2(rows, x), cnt, stride, RANK, rhs)
            cnt *= 2
            offset -= cnt
        offset += cnt
        state = [jnp.where(groups == 0, turned(x, -(o // 2) * rhs), 0.0) for o in range(octs)]
        cnt = 1
        while cnt < OCT:
            stride = OCT // cnt
            offset -= octs * cnt
            after = []
            for o in range(octs):
                x = state[o]
                if cnt > 1:
                    x = x + turned(x, stride * rhs)
                rows = down_ref[(offset + o * cnt) * RANK : (offset + (o + 1) * cnt) * RANK]
                after.append(pick(dot2(rows, x), cnt, stride, RANK, rhs))
            state = after
            cnt *= 2
        for o in range(octs):
            fields[o] = state[o] + turned(state[o], rhs)

    for u in range(EACH):
        o = g * EACH + u
        weights = []
        masks = [(groups == n).astype(f32).astype(bf16) for n in range(OCT)]
        for s in range(NF):
            w = None
            for n in range(OCT):
                entry = idx_ref[o * OCT + n, s]
                at = lut[lax.div(entry + leaves, leaves)] + jnp.bitwise_and(entry, leaves - 1)
                got = table[at] * masks[n]
                w = got if w is None else w + got
            weights.append(w)
        weights = jnp.concatenate(weights, 0)
        quarter = lane_group(8, 128, RANK)
        for n in range(OCT):
            c = coupling_ref[u * OCT + n].astype(f32)
            for t in range(8):
                shift[u, n, pl.ds(t, NF, stride=8), :] = c[:, t * 128 : (t + 1) * 128]
            for q in range(NF // 4):
                v = [shift[u, n, (q * 4 + s) * 8 : (q * 4 + s + 1) * 8, :] for s in range(4)]
                moved = []
                for a in range(4):
                    y = turned(v[0], (0 - a) * RANK)
                    for s in range(1, 4):
                        y = jnp.where(quarter == s, turned(v[s], (s - a) * RANK), y)
                    moved.append(y)
                lined[u, n * RANK : (n + 1) * RANK, q * 128 : (q + 1) * 128] = jnp.concatenate(moved, 0).astype(bf16)
        far = pick(jnp.dot(lined[u], weights, preferred_element_type=f32), OCT, 1, RANK, rhs)
        for a in range(4):
            far_at[u, pl.ds(a, 8, stride=4), :] = far[a * 8 : (a + 1) * 8]
        rows = down_ref[pl.ds(pl.multiple_of(o * OCT * RANK, OCT * RANK), OCT * RANK), :]
        field = far_at[u] + pick(dot2(rows, fields[o]), OCT, 1, RANK, rhs)
        field = field.T.astype(bf16)
        cols = slice(u * OCT * LEAF, (u + 1) * OCT * LEAF)
        got = lax.dot_general(field, basis_ref[cols, :], (((1,), (1,)), ((), ())), preferred_element_type=f32)
        out_ref[:, cols] = near_ref[:, cols] + pick(got, OCT, 1, rhs, LEAF)


def per_device(
    points, coords, basis, far_list, far_coupling, near_list, local_transfer, top_transfer, top_coupling
):
    rhs = points.shape[0]
    leaves = basis.shape[0]
    octs = leaves // OCT
    width = OCT * rhs
    size = leaves * LEAF
    count = lax.axis_size("leaf")
    bits = count.bit_length() - 1
    vmem = pl.BlockSpec(memory_space=pltpu.VMEM)
    smem = pl.BlockSpec(memory_space=pltpu.SMEM)
    limit = pltpu.CompilerParams(vmem_limit_bytes=48 * 2**20)

    def room(n):
        return -(-n // 16) * 16

    nodes = room(local_transfer.shape[0])
    coeff, top, down, brows = pl.pallas_call(
        functools.partial(up_kernel, rhs, octs),
        out_shape=(
            jax.ShapeDtypeStruct((RANK, leaves * rhs), bf16),
            jax.ShapeDtypeStruct((8, width), f32),
            jax.ShapeDtypeStruct((nodes * RANK, RANK), bf16),
            jax.ShapeDtypeStruct((size, RANK), bf16),
        ),
        in_specs=[vmem] * 3,
        out_specs=(vmem,) * 4,
        scratch_shapes=[
            pltpu.VMEM((nodes, RANK * RANK), f32),
            pltpu.VMEM((2, 8 * RANK, 128), f32),
            pltpu.VMEM((2, 64, 128), f32),
            pltpu.VMEM((leaves, LEAF * RANK), f32),
            pltpu.VMEM((2, OCT * LEAF, 128), f32),
            pltpu.VMEM((2, 128, 128), f32),
        ],
        compiler_params=limit,
        name="up",
    )(points, basis, local_transfer)

    total = count - 1 + 4 + bits
    ext_leaves = leaves + 2 * SPAN
    parts, tops, near_part = pl.pallas_call(
        functools.partial(near_kernel, count, bits, leaves, rhs),
        out_shape=(
            jax.ShapeDtypeStruct((bits + 1, RANK, leaves * rhs), bf16),
            jax.ShapeDtypeStruct((count, 8, width), f32),
            jax.ShapeDtypeStruct((rhs, size), f32),
        ),
        in_specs=[smem] + [vmem] * 4,
        out_specs=(vmem,) * 3,
        scratch_shapes=[
            pltpu.VMEM((8, size), f32),
            pltpu.VMEM((2, rhs, HALO), bf16),
            pltpu.VMEM((2, 8, HALO), f32),
            pltpu.VMEM((leaves, LEAF, 48), bf16),
            pltpu.VMEM((ext_leaves + 1, 48, 2 * LEAF), bf16),
            pltpu.VMEM((ext_leaves + 1, 48, 2 * LEAF), bf16),
            pltpu.VMEM((ext_leaves + 1, LEAF, rhs), bf16),
            pltpu.VMEM((leaves, LEAF, rhs), f32),
            pltpu.SemaphoreType.DMA((total,)),
            pltpu.SemaphoreType.DMA((total,)),
            pltpu.SemaphoreType.DMA((2,)),
        ],
        compiler_params=pltpu.CompilerParams(
            vmem_limit_bytes=48 * 2**20, collective_id=0, has_side_effects=True
        ),
        name="near",
    )(near_list, coeff, top, points, coords)

    whole = lambda *shape: pl.BlockSpec(shape, lambda g: (0,) * len(shape))
    return pl.pallas_call(
        functools.partial(far_kernel, count, bits, rhs, octs),
        grid=(octs // EACH,),
        out_shape=jax.ShapeDtypeStruct((rhs, size), f32),
        in_specs=[
            smem,
            pl.BlockSpec((EACH * OCT, NF, RANK * RANK), lambda g: (g, 0, 0)),
            whole(*parts.shape),
            whole(*tops.shape),
            whole(*top_transfer.shape),
            whole(*top_coupling.shape),
            whole(*down.shape),
            pl.BlockSpec((EACH * OCT * LEAF, RANK), lambda g: (g, 0)),
            pl.BlockSpec((rhs, EACH * OCT * LEAF), lambda g: (0, g)),
        ],
        out_specs=pl.BlockSpec((rhs, EACH * OCT * LEAF), lambda g: (0, g)),
        scratch_shapes=[
            pltpu.VMEM(((bits + 1) * leaves + 1, RANK, width), bf16),
            pltpu.VMEM((2 * count, RANK, width), f32),
            pltpu.VMEM((octs, RANK, width), f32),
            pltpu.VMEM((EACH, OCT, 8 * NF, 128), f32),
            pltpu.VMEM((EACH, OCT * RANK, NF * RANK), bf16),
            pltpu.VMEM((EACH, RANK, width), f32),
            pltpu.VMEM((room(top_transfer.shape[0]), RANK * RANK), f32),
            pltpu.VMEM((room(top_transfer.shape[0]) * RANK, 128), f32),
            pltpu.VMEM((room(2 * bits), RANK * RANK), f32),
            pltpu.VMEM((room(2 * bits) * RANK, 128), f32),
            pltpu.VMEM((bits, RANK, RANK), bf16),
            pltpu.VMEM((OCT, 64, 128), f32),
            pltpu.SMEM((count + 1,), jnp.int32),
        ],
        compiler_params=limit,
        name="far",
    )(far_list, far_coupling, parts, tops, top_transfer, top_coupling, down, brows, near_part)


def solution(mesh):
    return jax.shard_map(
        per_device,
        mesh=mesh,
        in_specs=(
            P(None, "leaf"),
            P(None, "leaf"),
            P("leaf", None),
            P("leaf", None),
            P("leaf", None, None),
            P("leaf", None),
            P("leaf", None),
            P(),
            P(),
        ),
        out_specs=P(None, "leaf"),
        check_vma=False,
    )
```

```python
import functools
import math

import jax
import jax.numpy as jnp
from jax import lax
from jax.experimental import pallas as pl
from jax.experimental.pallas import tpu as pltpu
from jax.sharding import PartitionSpec as P

LEAF = 64
RANK = 32
NF = 16
NN = 12
SPAN = 8
OCT = 8
HALO = SPAN * LEAF
GROUP = 8
EACH = 4
MESH = pl.DeviceIdType.MESH

variance = 1.0
nugget = 0.5
decay_rate = math.sqrt(3.0) / 0.3
f32 = jnp.float32
bf16 = jnp.bfloat16


def top_start(height, number):
    if height == 0:
        return 0
    return 2 * number - number // 2 ** (height - 1)


def halves(x):
    high = x.astype(bf16)
    return jnp.concatenate([high, (x - high.astype(f32)).astype(bf16)], 1)


def dot2(matrix, x, dims=((1,), (0,))):
    both = lax.dot_general(matrix, halves(x), (dims, ((), ())), preferred_element_type=f32)
    return both[:, : x.shape[1]] + both[:, x.shape[1] :]


def unfold(rows, work, out, base):
    tiles = rows.shape[1] // 128
    for t in range(tiles):
        work[pl.ds(t, 8, stride=tiles), :] = rows[:, t * 128 : (t + 1) * 128]
    for n in range(8 * tiles // 8):
        v = work[n * 8 : (n + 1) * 8, :]
        for q in range(4):
            out[pl.ds(base + n * 32 + q, 8, stride=4), :] = turned(v, -q * RANK)


def lane_group(rows, lanes, width):
    return lax.broadcasted_iota(jnp.int32, (rows, lanes), 1) // width


def pick(stacked, count, stride, rows, width):
    groups = lane_group(rows, stacked.shape[1], width)
    kept = jnp.zeros((rows, stacked.shape[1]), f32)
    for n in range(count):
        kept = jnp.where(groups == n * stride, stacked[n * rows : (n + 1) * rows], kept)
    return kept


def turned(x, shift):
    shift %= x.shape[1]
    return x if shift == 0 else pltpu.roll(x, shift, 1)


def up_kernel(
    rhs, octs, points_ref, basis_ref, local_ref, coeff_ref, top_ref, rows_ref, brows_ref,
    wide, spread_out, work, bwide, bout, bwork,
):
    width = OCT * rhs
    number = local_ref.shape[0]
    wide[0:number, :] = local_ref[...].astype(f32)
    bwide[...] = basis_ref[...].astype(f32)

    def open_local(block, carry):
        for u in range(4):
            rows = wide[pl.ds(pl.multiple_of((block * 4 + u) * 8, 8), 8), :]
            unfold(rows, work.at[u], spread_out.at[u], 0)
            at = pl.multiple_of((block * 4 + u) * 8 * RANK, 8 * RANK)
            rows_ref[pl.ds(at, 8 * RANK), :] = spread_out[u][:, :RANK].astype(bf16)
        return carry

    lax.fori_loop(0, wide.shape[0] // 32, open_local, 0)

    row = lax.broadcasted_iota(jnp.int32, (width, OCT * LEAF), 0) // rhs
    own = row == lane_group(width, OCT * LEAF, LEAF)
    state = []
    for g in range(octs):
        cols = slice(g * OCT * LEAF, (g + 1) * OCT * LEAF)
        unfold(bwide[g * OCT : (g + 1) * OCT, :], bwork.at[g % 2], bout.at[g % 2], 0)
        brows = bout[g % 2][:, :RANK].astype(bf16)
        brows_ref[cols, :] = brows
        x = points_ref[:, cols].astype(f32)
        spread = jnp.where(own, jnp.concatenate([x] * OCT, 0), 0.0).astype(bf16)
        c = jnp.dot(spread, brows, preferred_element_type=f32).T.astype(bf16)
        coeff_ref[:, g * width : (g + 1) * width] = c
        state.append(c.astype(f32))

    def apply(rows, x, count):
        mine = lax.broadcasted_iota(jnp.int32, (count * RANK, width), 0) // RANK * (OCT // count)
        tiled = jnp.where(mine == lane_group(count * RANK, width, rhs), jnp.concatenate([x] * count, 0), 0.0)
        return dot2(rows, tiled, ((0,), (0,)))

    offset = 0
    count = OCT
    while count >= 1:
        stride = OCT // count
        after = []
        for g in range(octs):
            rows = rows_ref[(offset + g * count) * RANK : (offset + (g + 1) * count) * RANK]
            kept = apply(rows, state[g], count)
            if count > 1:
                kept = kept + turned(kept, -stride * rhs)
            after.append(kept)
        state = after
        offset += octs * count
        count //= 2
    groups = lane_group(RANK, width, rhs)
    x = jnp.zeros((RANK, width), f32)
    for m in range(OCT):
        x = jnp.where(groups == m, turned(state[2 * m] + state[2 * m + 1], m * rhs), x)
    count = OCT
    while count > 1:
        stride = OCT // count
        rows = rows_ref[offset * RANK : (offset + count) * RANK]
        kept = apply(rows, x, count)
        x = kept + turned(kept, -stride * rhs)
        offset += count
        count //= 2
    small = lane_group(8, width, rhs)
    packed = jnp.zeros((8, width), f32)
    for m in range(RANK // 8):
        packed = jnp.where(small == m, turned(x[m * 8 : (m + 1) * 8], m * rhs), packed)
    top_ref[...] = packed


def near_kernel(
    count, bits, leaves, rhs, list_ref, coeff_ref, top_ref, points_ref, coords_ref,
    parts_ref, tops_ref, out_ref,
    wide, halo_points, halo_coords, p_ref, qa_ref, qb_ref, x_ref, acc, send_sem, recv_sem, own_sem,
):
    me = lax.axis_index("leaf")
    size = points_ref.shape[1]

    def other(step):
        return lax.rem(me + step, count)

    def flipped(b):
        return me + (1 << b) - 2 * (1 << b) * lax.rem(lax.div(me, 1 << b), 2)

    barrier = pltpu.get_barrier_semaphore()

    def greet(step, carry):
        pl.semaphore_signal(barrier, inc=1, device_id=(other(step),), device_id_type=MESH)
        return carry

    lax.fori_loop(1, count, greet, 0)
    wide[0:3, :] = coords_ref[...]
    wide[3:8, :] = jnp.zeros((5, size), f32)
    pl.semaphore_wait(barrier, count - 1)

    copies = []

    def send(src, dst, device):
        n = len(copies)
        copy = pltpu.make_async_remote_copy(
            src_ref=src, dst_ref=dst, send_sem=send_sem.at[n], recv_sem=recv_sem.at[n],
            device_id=(device,), device_id_type=MESH,
        )
        copy.start()
        copies.append(copy)

    left, right = other(count - 1), other(1)
    send(points_ref.at[:, pl.ds(size - HALO, HALO)], halo_points.at[0], right)
    send(points_ref.at[:, pl.ds(0, HALO)], halo_points.at[1], left)
    send(wide.at[:, pl.ds(size - HALO, HALO)], halo_coords.at[0], right)
    send(wide.at[:, pl.ds(0, HALO)], halo_coords.at[1], left)
    for b in reversed(range(bits)):
        send(coeff_ref, parts_ref.at[b + 1], flipped(b))
    for step in range(1, count):
        send(top_ref, tops_ref.at[step], other(step))
    own_copies = [
        pltpu.make_async_copy(coeff_ref, parts_ref.at[0], own_sem.at[0]),
        pltpu.make_async_copy(top_ref, tops_ref.at[0], own_sem.at[1]),
    ]
    for copy in own_copies:
        copy.start()

    empty = leaves + 2 * SPAN
    width = 2 * LEAF
    row = lax.broadcasted_iota(jnp.int32, (8, width), 0)
    low_half = lax.broadcasted_iota(jnp.int32, (48, width), 1) < LEAF
    origin = jnp.broadcast_to(wide[:, 0:width][:, :1], (8, width))

    def split(f):
        h = f.astype(bf16).astype(f32)
        m = (f - h).astype(bf16).astype(f32)
        return h, m, f - h - m

    def tables(b, own, pts, xyz):
        v = jnp.where(row < 3, decay_rate * (xyz - origin), 0.0)
        norm = jnp.sum(v * v, axis=0, keepdims=True)
        one = jnp.ones_like(v)
        h, m, l = split(jnp.where(row < 3, -2.0 * v, jnp.where(row == 3, norm, jnp.where(row == 4, one, 0.0))))
        q = jnp.concatenate([h, m, h, m, l, h], 0)
        r = pltpu.roll(q, LEAF, 1)
        qa_ref[2 * b] = jnp.where(low_half, q, 0.0).astype(bf16)
        qb_ref[2 * b] = jnp.where(low_half, 0.0, r).astype(bf16)
        qa_ref[2 * b + 1] = jnp.where(low_half, r, 0.0).astype(bf16)
        qb_ref[2 * b + 1] = jnp.where(low_half, 0.0, q).astype(bf16)
        x = pts.astype(f32).T.astype(bf16)
        x_ref[2 * b] = x[:LEAF]
        x_ref[2 * b + 1] = x[LEAF:]
        if own:
            h, m, l = split(jnp.where(row < 3, v, jnp.where(row == 3, one, jnp.where(row == 4, norm, 0.0))))
            p = jnp.concatenate([h, h, m, m, h, l], 0).T.astype(bf16)
            p_ref[2 * b - SPAN] = p[:LEAF]
            p_ref[2 * b + 1 - SPAN] = p[LEAF:]

    qa_ref[empty] = jnp.zeros(qa_ref.shape[1:], bf16)
    qb_ref[empty] = jnp.zeros(qb_ref.shape[1:], bf16)
    x_ref[empty] = jnp.zeros(x_ref.shape[1:], bf16)

    def own_tables(g, carry):
        for u in range(GROUP):
            b = g * GROUP + u
            cols = pl.ds(pl.multiple_of(b * width, width), width)
            tables(SPAN // 2 + b, True, points_ref[:, cols], wide[:, cols])
        return carry

    lax.fori_loop(0, leaves // 2 // GROUP, own_tables, 0)

    def leaf_product(leaf):
        t = []
        x = []
        for part in range(NN // 4):
            j = []
            for s in range(4):
                j.append(list_ref[leaf, part * 4 + s])
                x.append(x_ref[j[s]])
            q = jnp.concatenate([qa_ref[j[0]] + qb_ref[j[1]], qa_ref[j[2]] + qb_ref[j[3]]], axis=1)
            v = jnp.dot(p_ref[leaf], q, preferred_element_type=f32)
            v = jnp.maximum(v, 1e-12)
            r = v * lax.rsqrt(v)
            t.append(((1.0 + r) * jnp.exp(-r)).astype(bf16))
        return jnp.dot(jnp.concatenate(t, 1), jnp.concatenate(x, 0), preferred_element_type=f32)

    def group(g, carry):
        got = [leaf_product(g * GROUP + u) for u in range(GROUP)]
        for u in range(GROUP):
            leaf = g * GROUP + u
            acc[leaf] = got[u] + nugget * x_ref[leaf + SPAN].astype(f32)
        return carry

    lax.fori_loop(SPAN // GROUP, (leaves - SPAN) // GROUP, group, 0)
    for n in range(4):
        copies[n].wait()
    for side in range(2):
        for b in range(SPAN // 2):
            cols = slice(b * width, (b + 1) * width)
            at = b + side * (leaves + SPAN) // 2
            tables(at, False, halo_points[side, :, cols], halo_coords[side, :, cols])
    lax.fori_loop(0, SPAN // GROUP, group, 0)
    lax.fori_loop((leaves - SPAN) // GROUP, leaves // GROUP, group, 0)

    def turn(g, carry):
        for u in range(GROUP):
            b = g * GROUP + u
            block = acc[pl.ds(2 * b, 2)].reshape(width, rhs)
            out_ref[:, pl.ds(pl.multiple_of(b * width, width), width)] = block.T
        return carry

    lax.fori_loop(0, leaves // 2 // GROUP, turn, 0)
    for copy in own_copies:
        copy.wait()
    for copy in copies[4:]:
        copy.wait()


def far_kernel(
    count, bits, rhs, octs, idx_ref, coupling_ref, parts_ref, tops_ref, transfer_ref, cousins_ref,
    down_ref, basis_ref, near_ref, out_ref, table, levels, fields, shift, lined, far_at,
    wide, top_rows, picked, cousin_rows, step_rows, work,
):
    g = pl.program_id(0)
    width = OCT * rhs
    leaves = octs * OCT
    groups = lane_group(RANK, width, rhs)

    @pl.when(g == 0)
    def _():
        device = lax.axis_index("leaf")
        source = lax.broadcasted_iota(jnp.int32, (width, OCT * width), 0)
        target = lax.broadcasted_iota(jnp.int32, (width, OCT * width), 1)
        repeat = (source == target // width * rhs + target % rhs).astype(f32).astype(bf16)

        def fill(part, carry):
            for o in range(octs):
                block = parts_ref[part, :, o * width : (o + 1) * width]
                got = jnp.dot(block, repeat, preferred_element_type=f32).astype(bf16)
                for n in range(OCT):
                    table[(part * octs + o) * OCT + n] = got[:, n * width : (n + 1) * width]
            return carry

        lax.fori_loop(0, bits + 1, fill, 0)
        table[(bits + 1) * leaves] = jnp.zeros((RANK, width), bf16)

        for step in range(count):
            packed = tops_ref[step]
            whole = jnp.concatenate([turned(packed, -m * rhs) for m in range(RANK // 8)], 0)
            levels[lax.rem(device - step + count, count)] = whole
        wide[0 : transfer_ref.shape[0], :] = transfer_ref[...].astype(f32)
        blocks = wide.shape[0] // 8
        for b in range(blocks):
            unfold(wide[b * 8 : (b + 1) * 8, :], work.at[b % OCT], top_rows, b * 8 * RANK)
        for height in range(bits - 1):
            at = top_start(height, count) + lax.div(device, 1 << height)
            picked[2 * height : 2 * height + 2, :] = cousins_ref[at].astype(f32)
            steps = top_rows[pl.ds(pl.multiple_of(at * RANK, RANK), RANK), :][:, :RANK]
            step_rows[height] = steps.astype(bf16)
        for b in range(picked.shape[0] // 8):
            unfold(picked[b * 8 : (b + 1) * 8, :], work.at[b % OCT], cousin_rows, b * 8 * RANK)
        number, base = count, 0
        for height in range(bits - 2):
            start = top_start(height, count)
            for m in range(number // 2):
                both = jnp.concatenate([levels[base + 2 * m], levels[base + 2 * m + 1]], 0)
                at = (start + 2 * m) * RANK
                two = top_rows[at : at + 2 * RANK, :][:, :RANK].astype(bf16)
                levels[base + number + m] = dot2(two, both, ((0,), (0,)))
            base += number
            number //= 2
        field = None
        for height in range(bits - 2, -1, -1):
            base = 2 * count - 2 * (count >> height)
            uncle = lax.rem(lax.div(device, 2 << height) + 1, 2) + 2 * lax.div(device, 4 << height)
            term = 0.0
            for side in range(2):
                at = (2 * height + side) * RANK
                matrix = cousin_rows[at : at + RANK, :][:, :RANK].astype(bf16)
                term = term + dot2(matrix, levels[base + 2 * uncle + side])
            field = term if field is None else term + dot2(step_rows[height], field)
        x = jnp.where(groups == 0, field, 0.0)
        offset = 2 * leaves - 4
        cnt = 2
        while cnt <= OCT:
            stride = OCT // cnt
            x = x + turned(x, stride * rhs)
            rows = down_ref[offset * RANK : (offset + cnt) * RANK]
            x = pick(dot2(rows, x), cnt, stride, RANK, rhs)
            cnt *= 2
            offset -= cnt
        offset += cnt
        state = [jnp.where(groups == 0, turned(x, -(o // 2) * rhs), 0.0) for o in range(octs)]
        cnt = 1
        while cnt < OCT:
            stride = OCT // cnt
            offset -= octs * cnt
            after = []
            for o in range(octs):
                x = state[o]
                if cnt > 1:
                    x = x + turned(x, stride * rhs)
                rows = down_ref[(offset + o * cnt) * RANK : (offset + (o + 1) * cnt) * RANK]
                after.append(pick(dot2(rows, x), cnt, stride, RANK, rhs))
            state = after
            cnt *= 2
        for o in range(octs):
            fields[o] = state[o] + turned(state[o], rhs)

    for u in range(EACH):
        o = g * EACH + u
        weights = []
        masks = [(groups == n).astype(f32).astype(bf16) for n in range(OCT)]
        for s in range(NF):
            w = None
            for n in range(OCT):
                got = table[idx_ref[o * OCT + n, s]] * masks[n]
                w = got if w is None else w + got
            weights.append(w)
        weights = jnp.concatenate(weights, 0)
        quarter = lane_group(8, 128, RANK)
        for n in range(OCT):
            c = coupling_ref[u * OCT + n].astype(f32)
            for t in range(8):
                shift[u, n, pl.ds(t, NF, stride=8), :] = c[:, t * 128 : (t + 1) * 128]
            for q in range(NF // 4):
                v = [shift[u, n, (q * 4 + s) * 8 : (q * 4 + s + 1) * 8, :] for s in range(4)]
                moved = []
                for a in range(4):
                    y = turned(v[0], (0 - a) * RANK)
                    for s in range(1, 4):
                        y = jnp.where(quarter == s, turned(v[s], (s - a) * RANK), y)
                    moved.append(y)
                lined[u, n * RANK : (n + 1) * RANK, q * 128 : (q + 1) * 128] = jnp.concatenate(moved, 0).astype(bf16)
        far = pick(jnp.dot(lined[u], weights, preferred_element_type=f32), OCT, 1, RANK, rhs)
        for a in range(4):
            far_at[u, pl.ds(a, 8, stride=4), :] = far[a * 8 : (a + 1) * 8]
        rows = down_ref[pl.ds(pl.multiple_of(o * OCT * RANK, OCT * RANK), OCT * RANK), :]
        field = far_at[u] + pick(dot2(rows, fields[o]), OCT, 1, RANK, rhs)
        field = field.T.astype(bf16)
        cols = slice(u * OCT * LEAF, (u + 1) * OCT * LEAF)
        got = lax.dot_general(field, basis_ref[cols, :], (((1,), (1,)), ((), ())), preferred_element_type=f32)
        out_ref[:, cols] = near_ref[:, cols] + pick(got, OCT, 1, rhs, LEAF)


def per_device(
    points, coords, basis, far_list, far_coupling, near_list, local_transfer, top_transfer, top_coupling
):
    rhs = points.shape[0]
    leaves = basis.shape[0]
    octs = leaves // OCT
    width = OCT * rhs
    size = leaves * LEAF
    device = lax.axis_index("leaf")
    count = lax.axis_size("leaf")
    bits = count.bit_length() - 1
    vmem = pl.BlockSpec(memory_space=pltpu.VMEM)
    smem = pl.BlockSpec(memory_space=pltpu.SMEM)
    limit = pltpu.CompilerParams(vmem_limit_bytes=48 * 2**20)

    def room(n):
        return -(-n // 32) * 32

    nodes = room(local_transfer.shape[0])
    coeff, top, down, brows = pl.pallas_call(
        functools.partial(up_kernel, rhs, octs),
        out_shape=(
            jax.ShapeDtypeStruct((RANK, leaves * rhs), bf16),
            jax.ShapeDtypeStruct((8, width), f32),
            jax.ShapeDtypeStruct((nodes * RANK, RANK), bf16),
            jax.ShapeDtypeStruct((size, RANK), bf16),
        ),
        in_specs=[vmem] * 3,
        out_specs=(vmem,) * 4,
        scratch_shapes=[
            pltpu.VMEM((nodes, RANK * RANK), f32),
            pltpu.VMEM((4, 8 * RANK, 128), f32),
            pltpu.VMEM((4, 64, 128), f32),
            pltpu.VMEM((leaves, LEAF * RANK), f32),
            pltpu.VMEM((2, OCT * LEAF, 128), f32),
            pltpu.VMEM((2, 128, 128), f32),
        ],
        compiler_params=limit,
        name="up",
    )(points, basis, local_transfer)

    total = count - 1 + 4 + bits
    ext_leaves = leaves + 2 * SPAN
    near_idx = jnp.where(near_list >= 0, near_list - device * leaves + SPAN, ext_leaves)
    apart = jnp.bitwise_xor(jnp.right_shift(far_list, leaves.bit_length() - 1), device)
    place = sum(jnp.where(apart == 1 << b, (b + 1) * leaves, 0) for b in range(bits))
    far_idx = place + jnp.bitwise_and(far_list, leaves - 1)
    far_idx = jnp.where(far_list >= 0, far_idx, (bits + 1) * leaves)
    parts, tops, near_part = pl.pallas_call(
        functools.partial(near_kernel, count, bits, leaves, rhs),
        out_shape=(
            jax.ShapeDtypeStruct((bits + 1, RANK, leaves * rhs), bf16),
            jax.ShapeDtypeStruct((count, 8, width), f32),
            jax.ShapeDtypeStruct((rhs, size), f32),
        ),
        in_specs=[smem] + [vmem] * 4,
        out_specs=(vmem,) * 3,
        scratch_shapes=[
            pltpu.VMEM((8, size), f32),
            pltpu.VMEM((2, rhs, HALO), bf16),
            pltpu.VMEM((2, 8, HALO), f32),
            pltpu.VMEM((leaves, LEAF, 48), bf16),
            pltpu.VMEM((ext_leaves + 1, 48, 2 * LEAF), bf16),
            pltpu.VMEM((ext_leaves + 1, 48, 2 * LEAF), bf16),
            pltpu.VMEM((ext_leaves + 1, LEAF, rhs), bf16),
            pltpu.VMEM((leaves, LEAF, rhs), f32),
            pltpu.SemaphoreType.DMA((total,)),
            pltpu.SemaphoreType.DMA((total,)),
            pltpu.SemaphoreType.DMA((2,)),
        ],
        compiler_params=pltpu.CompilerParams(
            vmem_limit_bytes=48 * 2**20, collective_id=0, has_side_effects=True
        ),
        name="near",
    )(near_idx, coeff, top, points, coords)

    whole = lambda *shape: pl.BlockSpec(shape, lambda g: (0,) * len(shape))
    return pl.pallas_call(
        functools.partial(far_kernel, count, bits, rhs, octs),
        grid=(octs // EACH,),
        out_shape=jax.ShapeDtypeStruct((rhs, size), f32),
        in_specs=[
            smem,
            pl.BlockSpec((EACH * OCT, NF, RANK * RANK), lambda g: (g, 0, 0)),
            whole(*parts.shape),
            whole(*tops.shape),
            whole(*top_transfer.shape),
            whole(*top_coupling.shape),
            whole(*down.shape),
            pl.BlockSpec((EACH * OCT * LEAF, RANK), lambda g: (g, 0)),
            pl.BlockSpec((rhs, EACH * OCT * LEAF), lambda g: (0, g)),
        ],
        out_specs=pl.BlockSpec((rhs, EACH * OCT * LEAF), lambda g: (0, g)),
        scratch_shapes=[
            pltpu.VMEM(((bits + 1) * leaves + 1, RANK, width), bf16),
            pltpu.VMEM((2 * count, RANK, width), f32),
            pltpu.VMEM((octs, RANK, width), f32),
            pltpu.VMEM((EACH, OCT, 8 * NF, 128), f32),
            pltpu.VMEM((EACH, OCT * RANK, NF * RANK), bf16),
            pltpu.VMEM((EACH, RANK, width), f32),
            pltpu.VMEM((room(top_transfer.shape[0]), RANK * RANK), f32),
            pltpu.VMEM((room(top_transfer.shape[0]) * RANK, 128), f32),
            pltpu.VMEM((room(2 * bits), RANK * RANK), f32),
            pltpu.VMEM((room(2 * bits) * RANK, 128), f32),
            pltpu.VMEM((bits, RANK, RANK), bf16),
            pltpu.VMEM((OCT, 64, 128), f32),
        ],
        compiler_params=limit,
        name="far",
    )(far_idx, far_coupling, parts, tops, top_transfer, top_coupling, down, brows, near_part)


def solution(mesh):
    return jax.shard_map(
        per_device,
        mesh=mesh,
        in_specs=(
            P(None, "leaf"),
            P(None, "leaf"),
            P("leaf", None),
            P("leaf", None),
            P("leaf", None, None),
            P("leaf", None),
            P("leaf", None),
            P(),
            P(),
        ),
        out_specs=P(None, "leaf"),
        check_vma=False,
    )
```
